128 devices in a mesh: section: 2 (over x_lo), dp: 4 (over x_hi, core), ctx: 16 (over y, z).
Axes of the slice: x: 4 (x_hi: 2, x_lo: 2; x = x_hi * 2 + x_lo), y: 4, z: 4, core: 2. Of those that a mesh axis runs over, the one named last changes fastest.
Arguments:
- inputs: bfloat16 [8, 1024, 1536], P('dp', 'ctx'), may hold values from -6 to 6
- cotangent: bfloat16 [8, 1024, 1536], P('dp', 'ctx'), may hold values from -6 to 6
- positions: int32 [8, 1024], P('dp'), may hold values from 0 to 1023, each once within a row
- granularity: int32 [8], P('dp'), may hold values from 0 to 3, as said below
- attention_gain: bfloat16 [2, 1536], P('section', ('dp', 'ctx')), may hold values from 0.25 to 1.75
- attention_in: bfloat16 [2, 1536, 4608], P('section', ('dp', 'ctx')), may hold values from -0.15625 to 0.15625
- attention_out: bfloat16 [2, 1536, 1536], P('section', ('dp', 'ctx')), may hold values from -2.5 to 2.5
- feed_gain: bfloat16 [2, 1536], P('section', ('dp', 'ctx')), may hold values from 0.25 to 1.75
- feed_up: bfloat16 [2, 1536, 6144], P('section', ('dp', 'ctx')), may hold values from -0.15625 to 0.15625
- feed_down: bfloat16 [2, 6144, 1536], P('section', ('dp', 'ctx')), may hold values from -0.15625 to 0.15625
Outputs:
- hidden: bfloat16 [2, 8, 1024, 1536], P('section', 'dp', 'ctx')
- input_grads: bfloat16 [2, 8, 1024, 1536], P('section', 'dp', 'ctx')
- grad_attention_gain: float32 [2, 1536], P('section', ('dp', 'ctx'))
- grad_attention_in: float32 [2, 1536, 4608], P('section', ('dp', 'ctx'))
- grad_attention_out: float32 [2, 1536, 1536], P('section', ('dp', 'ctx'))
- grad_feed_gain: float32 [2, 1536], P('section', ('dp', 'ctx'))
- grad_feed_up: float32 [2, 1536, 6144], P('section', ('dp', 'ctx'))
- grad_feed_down: float32 [2, 6144, 1536], P('section', ('dp', 'ctx'))
The draws below stay inside these ranges and needn't reach their ends.
Inputs may be any that keep to these rules, and one draw needn't show every extreme that they name: Each row of positions holds every position of its sequence once. The feed-forward of a micro-batch uses 6144 // 8 * 2 ** granularity hidden units.
All inputs are finite; a program needn't handle non-finite values.
Results may differ from the reference program's by a relative error of at most 0.022.
Values may be sent and summed in bfloat16 or wider, within the bound.
No kernel may reach another device: no remote copies, remote signals or barrier semaphores. Data moves between devices by JAX's collectives and lax.ppermute only.
A program may use at most 512 MiB of HBM per device.

```python
import math
import jax
import jax.numpy as jnp
from jax import lax

D = 1536
HEAD = 128
FF = 6144
SEQ_LEN = 1024
SEQ_MB = 1
LAYERS = 2
MICROS = 8
SEQS = 8


def draw_granularity(key, part):
    key = jax.random.fold_in(key, 5)
    total_micro = MICROS
    levels = jax.random.randint(jax.random.fold_in(key, 1), (total_micro,), 0, 4)
    top_spot = jax.random.randint(jax.random.fold_in(key, 2), (), 0, total_micro)
    low_spot = (top_spot + 1 + jax.random.randint(jax.random.fold_in(key, 3), (), 0, total_micro - 1)) % total_micro
    places = jnp.arange(total_micro)
    levels = jnp.where(places == top_spot, 3, levels)
    levels = jnp.where(places == low_spot, 0, levels)
    return levels.astype(jnp.int32)


def block_scale(key, extent, split, least, largest):
    loudness, own = 1.0, jax.random.fold_in(key, 6)
    for position, shards_of in split:
        steps = jnp.exp(jax.random.uniform(jax.random.fold_in(own, position), (shards_of,), jnp.float32, least / len(split), largest / len(split)))
        loudness = loudness * jnp.repeat(steps, extent[position] // shards_of).reshape([-1 if axis == position else 1 for axis in range(len(extent))])
    return loudness


def noise(key, shape, deviation, most, shards=(), kind=jnp.bfloat16):
    loudness = block_scale(key, shape, shards, -0.22, 0.18) if shards else 1.0
    result = jax.random.normal(key, shape, jnp.float32) * deviation * loudness
    return jnp.minimum(jnp.maximum(result, -most), most).astype(kind)


def setup_inputs(seed: int = 0) -> dict:
    arg_keys = jax.random.split(jax.random.key(seed), 11)
    return {
        "inputs": noise(arg_keys[0], (SEQS, SEQ_LEN, D), 1.0, 6.0, ((0, 4), (1, 16))),
        "cotangent": noise(arg_keys[1], (SEQS, SEQ_LEN, D), 1.0, 6.0, ((0, 4), (1, 16))),
        "positions": jax.vmap(lambda own: jax.random.permutation(own, SEQ_LEN))(jax.random.split(arg_keys[2], SEQS)).reshape((SEQS, SEQ_LEN)).astype(jnp.int32),
        "granularity": draw_granularity(jax.random.fold_in(arg_keys[10], 71), 0),
        "attention_gain": jnp.clip(1.0 + 0.15 * jax.random.normal(arg_keys[4], (LAYERS, D), jnp.float32), 0.25, 1.75).astype(jnp.bfloat16),
        "attention_in": noise(arg_keys[5], (LAYERS, D, 3 * D), D ** -0.5, 0.15625, ((0, 2), (1, 64))),
        "attention_out": noise(arg_keys[6], (LAYERS, D, D), (max(D // 256, 1)) ** -0.5, 2.5, ((0, 2), (1, 64))),
        "feed_gain": jnp.clip(1.0 + 0.15 * jax.random.normal(arg_keys[7], (LAYERS, D), jnp.float32), 0.25, 1.75).astype(jnp.bfloat16),
        "feed_up": noise(arg_keys[8], (LAYERS, D, FF), D ** -0.5, 0.15625, ((0, 2), (1, 64))),
        "feed_down": noise(arg_keys[9], (LAYERS, FF, D), (FF // 4) ** -0.5, 0.15625, ((0, 2), (1, 64))),
    }


EPS = 1e-05
THETA = 10000.0
MASKED = -1e+30

@jax.custom_vjp
def low(v):
    return lax.optimization_barrier(v.astype(jnp.bfloat16)).astype(jnp.float32)

@jax.custom_vjp
def low_back(v):
    return v

def low_keep(v):
    return (low(v), None)

def low_pass(kept, grad):
    return (grad,)

def back_keep(v):
    return (v, None)

def back_low(kept, grad):
    return (low(grad),)
low.defvjp(low_keep, low_pass)
low_back.defvjp(back_keep, back_low)

def rotary_angles(pos_rows, half_size):
    freqs = jnp.exp(-math.log(THETA) * jnp.arange(half_size, dtype=jnp.float32) / half_size)
    angles = pos_rows.astype(jnp.float32)[..., None] * freqs
    return (jnp.cos(angles)[..., None, :], jnp.sin(angles)[..., None, :])

def rotate(vectors, cosines, sine_table):
    half_size = vectors.shape[-1] // 2
    first_half, second_half = (vectors[..., :half_size], vectors[..., half_size:])
    return jnp.concatenate([first_half * cosines - second_half * sine_table, second_half * cosines + first_half * sine_table], -1)

def highest(left_side, right_side):
    return jnp.dot(left_side, right_side, precision=lax.Precision.HIGHEST)

def norm_scale(stream):
    return lax.rsqrt(lax.optimization_barrier(jnp.mean(stream * stream, -1, keepdims=True)) + EPS)

def layer_apply(stream, pos_rows, unit_mask, attention_gain, attention_in, attention_out, feed_gain, feed_up, feed_down):
    seq_length, model_width = stream.shape
    head_count = model_width // HEAD
    score_scale = 1.0 / math.sqrt(HEAD)
    normed = low(stream * norm_scale(stream) * attention_gain)
    projected = low_back(highest(normed, attention_in))
    cosines, sine_table = rotary_angles(pos_rows, HEAD // 2)
    queries = low(rotate(projected[:, :model_width].reshape(seq_length, head_count, HEAD), cosines, sine_table))
    keys_all = low(rotate(projected[:, model_width:2 * model_width].reshape(seq_length, head_count, HEAD), cosines, sine_table))
    values_all = low(projected[:, 2 * model_width:].reshape(seq_length, head_count, HEAD))
    block_rows = min(512, seq_length)

    def attend(block_args):
        q_block, p_block = block_args
        scores = jnp.einsum('qhd,khd->hqk', q_block, keys_all, precision=lax.Precision.HIGHEST) * score_scale
        scores = low_back(scores)
        scores = jnp.where(pos_rows[None, None, :] <= p_block[None, :, None], scores, MASKED)
        row_max = lax.optimization_barrier(jnp.max(scores, -1, keepdims=True))
        exponent = jnp.exp(scores - row_max)
        attn_probs = low(exponent / lax.optimization_barrier(jnp.sum(exponent, -1, keepdims=True)))
        return jnp.einsum('hqk,khd->qhd', attn_probs, values_all, precision=lax.Precision.HIGHEST)
    combined = lax.map(jax.checkpoint(attend), (queries.reshape(seq_length // block_rows, block_rows, head_count, HEAD), pos_rows.reshape(seq_length // block_rows, block_rows)))
    combined = low(low_back(combined.reshape(seq_length, model_width)))
    middle = stream + low_back(highest(combined, attention_out))
    normed_two = low(middle * norm_scale(middle) * feed_gain)
    up_proj = low_back(highest(normed_two, feed_up))
    hidden = low(jax.nn.gelu(up_proj, approximate=False) * unit_mask)
    return middle + low_back(highest(hidden, feed_down))

def reference(inputs, cotangent, positions, granularity, attention_gain, attention_in, attention_out, feed_gain, feed_up, feed_down):
    widths_table = jnp.array([FF // 8, FF // 4, FF // 2, FF], jnp.int32)
    seq_total = inputs.shape[0]
    widths = widths_table[granularity][jnp.arange(seq_total) // SEQ_MB]
    unit_masks = (jnp.arange(FF)[None, :] < widths[:, None]).astype(jnp.float32)
    params = tuple((weight.astype(jnp.float32) for weight in (attention_gain, attention_in, attention_out, feed_gain, feed_up, feed_down)))
    inputs_f = inputs.astype(jnp.float32)
    zero_shifts = jnp.zeros((LAYERS,) + inputs.shape, jnp.float32)

    def forward(shifts, gain_one, weight_in, weight_out, gain_two, weight_up, weight_down):

        def per_seq(carry_in, seq_item):
            stream, shift_seq, pos_rows, unit_mask = seq_item
            per_layer = []
            for layer_index in range(LAYERS):
                stream = stream + shift_seq[layer_index]
                stream = layer_apply(stream, pos_rows, unit_mask, gain_one[layer_index], weight_in[layer_index], weight_out[layer_index], gain_two[layer_index], weight_up[layer_index], weight_down[layer_index])
                stream = low(low_back(stream))
                per_layer.append(stream)
            return (carry_in, jnp.stack(per_layer))
        _, stacked = lax.scan(per_seq, jnp.zeros((), jnp.float32), (inputs_f, jnp.swapaxes(shifts, 0, 1), positions, unit_masks))
        return jnp.swapaxes(stacked, 0, 1)
    hidden, pullback = jax.vjp(forward, zero_shifts, *params)
    seed_ct = jnp.zeros_like(hidden).at[LAYERS - 1].set(cotangent.astype(jnp.float32))
    grads_all = pullback(seed_ct)
    return (hidden.astype(jnp.bfloat16), grads_all[0].astype(jnp.bfloat16), grads_all[1], grads_all[2], grads_all[3], grads_all[4], grads_all[5], grads_all[6])
```

```python
import math

import jax
import jax.numpy as jnp
from jax import lax
from jax.experimental import pallas as pl
from jax.experimental.pallas import tpu as pltpu
from jax.sharding import Mesh
from jax.sharding import PartitionSpec as P

HEAD = 128
EPS = 1e-05
THETA = 10000.0
MASKED = -1e30
BF = jnp.bfloat16
F32 = jnp.float32
PLANE = ("xh", "core", "y")
EVERY = ("sec", "xh", "core", "y", "z")


def shifted(block, axis, distance):
    n = lax.axis_size(axis)
    return lax.ppermute(block, axis, [(i, (i + distance) % n) for i in range(n)])


def gather_ring(block, axis):
    return [block] + [shifted(block, axis, k) for k in range(1, lax.axis_size(axis))]


def gathered(block, axis):
    return jnp.concatenate(gather_ring(block, axis), 0)


def scattered(blocks, axis):
    total = blocks[0].astype(F32)
    for k in range(1, lax.axis_size(axis)):
        total = total + shifted(blocks[k].astype(BF), axis, -k).astype(F32)
    return total


def rolled(array, axis_name, dim):
    n = lax.axis_size(axis_name)
    me = lax.axis_index(axis_name)
    return jnp.concatenate(
        [lax.dynamic_slice_in_dim(array, lax.rem(me - k + n, n), 1, dim) for k in range(n)], dim
    )


def family(block):
    near = shifted(block, "core", 1)
    far = shifted(block, "sec", 1)
    return jnp.concatenate([block, near, far, shifted(far, "core", 1)], 0)


def place(sec, core, y):
    return (sec * 2 + core) * 4 + y


def brought(pair):
    got = []
    for i in (0, 1):
        route = [
            (place(y // 2, core, y), place(y // 2, y % 2, 2 * core + i))
            for core in (0, 1)
            for y in range(4)
        ]
        got.append(lax.ppermute(pair[i], ("sec", "core", "y"), route))
    return jnp.where(lax.axis_index("y") % 2 == 0, got[0], got[1])


def returned(block, layer):
    got = []
    for i in (0, 1):
        route = [
            (place(sec, core, y), place(layer, y // 2, 2 * sec + core))
            for sec in (0, 1)
            for core in (0, 1)
            for y in (i, i + 2)
        ]
        got.append(lax.ppermute(block, ("sec", "core", "y"), route))
    return jnp.stack(got)


def dot(a, b):
    return jnp.dot(a, b, preferred_element_type=F32)


def dot_t(a, b):
    return lax.dot_general(a, b, (((1,), (1,)), ((), ())), preferred_element_type=F32)


def t_dot(a, b):
    return lax.dot_general(a, b, (((0,), (0,)), ((), ())), preferred_element_type=F32)


def norm_scale(v):
    return lax.rsqrt(jnp.mean(v * v, -1, keepdims=True) + EPS)


def gelu_parts(up):
    phi = 0.5 + 0.5 * lax.erf(up * math.sqrt(0.5))
    density = jnp.exp(-0.5 * up * up) * (1.0 / math.sqrt(2.0 * math.pi))
    return up * phi, phi + up * density


def tied(*arrays):
    return lax.optimization_barrier(arrays)


VMEM = pl.BlockSpec(memory_space=pltpu.VMEM)
SMEM = pl.BlockSpec(memory_space=pltpu.SMEM)


def costs(flops, arrays):
    moved = sum(math.prod(a.shape) * jnp.dtype(a.dtype).itemsize for a in arrays)
    return pl.CostEstimate(flops=int(flops), bytes_accessed=int(moved), transcendentals=0)


def call(kernel, out_shape, flops, here, *args, halves):
    return pl.pallas_call(
        kernel,
        out_shape=out_shape,
        in_specs=[SMEM] + [VMEM] * len(args) + [pl.BlockSpec(memory_space=pl.ANY)] * 2,
        out_specs=[VMEM] * len(out_shape),
        scratch_shapes=fetch_scratch(halves),
        compiler_params=pltpu.CompilerParams(vmem_limit_bytes=56 * 2**20),
        cost_estimate=costs(flops, [*args, *halves, *out_shape]),
    )(here, *args, *halves)


def shape(dims, dtype):
    return jax.ShapeDtypeStruct(dims, dtype)


def part_shapes(features):
    return [shape((64, features), F32)] + [shape((64, features), BF)] * 3


def store_parts(total, refs):
    for k, ref in enumerate(refs):
        ref[...] = total[64 * k : 64 * (k + 1)].astype(ref.dtype)


def summed(parts, received):
    total = parts[0].astype(F32)
    for r in received:
        total = total + r.astype(F32)
    return total


def sent_home(parts):
    return [shifted(parts[k], "z", -k) for k in range(1, 4)]


def swap_halves(v):
    return pltpu.roll(v, HEAD // 2, 1)


def fetches(here_ref, mine_ref, other_ref, whole, sems):
    core = here_ref[0]
    block = mine_ref.shape[1]
    copies = []
    for xh in (0, 1):
        for i, (ref, c) in enumerate(((mine_ref, core), (other_ref, 1 - core))):
            at = pl.multiple_of((2 * xh + c) * block, 16)
            copy = pltpu.make_async_copy(ref.at[xh], whole.at[pl.ds(at, block)], sems.at[2 * xh + i])
            copy.start()
            copies.append(copy)
    return copies


def fetched(copies):
    for copy in copies:
        copy.wait()


def fetch_scratch(halves):
    rows, columns = halves[0].shape[1:]
    return [pltpu.VMEM((4 * rows, columns), BF), pltpu.SemaphoreType.DMA((4,))]


def qkv_kernel(here_ref, n_ref, cos_ref, sin_ref, mine_ref, other_ref, q_ref, kv_ref, whole, sems):
    fetched(fetches(here_ref, mine_ref, other_ref, whole, sems))
    width = q_ref.shape[1]
    cos, sin = cos_ref[...], sin_ref[...]
    for j in (0, 1, 2):
        ref, at = (q_ref, 0) if j == 0 else (kv_ref, (j - 1) * width)
        total = dot(n_ref[...], whole[:, j * width : (j + 1) * width])
        for h in range(0, width, HEAD):
            v = total[:, h : h + HEAD]
            if j < 2:
                v = v * cos + swap_halves(v) * sin
            ref[:, at + h : at + h + HEAD] = v.astype(BF)


def masked_scores(q, k, visible):
    return jnp.where(visible, dot_t(q, k) * (1.0 / math.sqrt(HEAD)), MASKED)


def attend_kernel(
    here_ref, q_ref, kv_ref, pq_ref, pk_ref, mine_ref, other_ref, mixed_ref, lse_ref, *refs
):
    *part_refs, whole, sems = refs
    copies = fetches(here_ref, mine_ref, other_ref, whole, sems)
    width = q_ref.shape[1]
    visible = pk_ref[...] <= pq_ref[...]
    for i in range(width // HEAD):
        h = slice(i * HEAD, (i + 1) * HEAD)
        scores = masked_scores(q_ref[:, h], kv_ref[:, h], visible)
        most = jnp.max(scores, -1, keepdims=True)
        exponent = jnp.exp(scores - most)
        total = jnp.sum(exponent, -1, keepdims=True)
        probs = (exponent / total).astype(BF)
        values = kv_ref[:, width + i * HEAD : width + (i + 1) * HEAD]
        mixed_ref[:, h] = dot(probs, values).astype(BF)
        lse_ref[:, h] = jnp.broadcast_to(most + jnp.log(total), (q_ref.shape[0], HEAD))
    fetched(copies)
    store_parts(dot(mixed_ref[...], whole[...]), part_refs)


def attend_back_kernel(
    here_ref, b_ref, q_ref, kv_ref, lse_ref, pq_ref, pk_ref, cos_ref, sin_ref, mine_ref, other_ref,
    dq_ref, own_ref, send_ref, far_ref, whole, sems,
):
    fetched(fetches(here_ref, mine_ref, other_ref, whole, sems))
    tokens, width = q_ref.shape
    scale = 1.0 / math.sqrt(HEAD)
    visible = pk_ref[...] <= pq_ref[...]
    grad_mixed = dot_t(b_ref[...], whole[...]).astype(BF)
    for i in range(width // HEAD):
        h = slice(i * HEAD, (i + 1) * HEAD)
        vh = slice(width + i * HEAD, width + (i + 1) * HEAD)
        q, k, v, g = q_ref[:, h], kv_ref[:, h], kv_ref[:, vh], grad_mixed[:, h]
        probs = jnp.exp(masked_scores(q, k, visible) - lse_ref[:, i * HEAD : i * HEAD + 1])
        grad_probs = dot_t(g, v)
        weighted = jnp.sum(probs * grad_probs, -1, keepdims=True)
        grad_scores = (probs * (grad_probs - weighted)).astype(BF)
        dq = dot(grad_scores, k) * scale
        dq_ref[:, h] = (dq * cos_ref[...] - swap_halves(dq) * sin_ref[...]).astype(BF)
        for lanes, grad in (
            (h, t_dot(grad_scores, q) * scale),
            (vh, t_dot(probs.astype(BF), g)),
        ):
            own_ref[:, lanes] = grad[:tokens]
            send_ref[:tokens, lanes] = grad[tokens : 2 * tokens].astype(BF)
            far_ref[:, lanes] = grad[2 * tokens : 3 * tokens]
            send_ref[tokens:, lanes] = grad[3 * tokens :].astype(BF)


def project_back_kernel(
    here_ref, dq_ref, own_ref, near_ref, far_ref, cos_ref, sin_ref, mine_ref, other_ref,
    grad_ref, *refs,
):
    *part_refs, whole, sems = refs
    copies = fetches(here_ref, mine_ref, other_ref, whole, sems)
    width = dq_ref.shape[1]
    grad_ref[:, :width] = dq_ref[...]
    for h in range(0, 2 * width, HEAD):
        lanes = slice(h, h + HEAD)
        v = own_ref[:, lanes] + near_ref[:, lanes].astype(F32) + far_ref[:, lanes].astype(F32)
        if h < width:
            v = v * cos_ref[...] - swap_halves(v) * sin_ref[...]
        grad_ref[:, width + h : width + h + HEAD] = v.astype(BF)
    fetched(copies)
    store_parts(dot_t(grad_ref[...], whole[...]), part_refs)


def block_grads(refs):
    for i in range(len(refs) // 4):
        left, left_near, right, right_near = refs[4 * i : 4 * i + 4]
        total = t_dot(left[...], right[...]) + t_dot(left_near[...], right_near[...])
        yield i, total.reshape(4, total.shape[0] // 4, total.shape[1])


def weight_grad_kernel(here_ref, *refs):
    (out_ref,) = refs[-1:]
    for _, total in block_grads(refs[:-1]):
        out_ref[:, 0] = total.astype(BF)


def weight_grad_ring_kernel(here_ref, *refs):
    *refs, o0, o1, o2, o3, hold = refs
    rows = hold.shape[1]
    for i, total in block_grads(refs):
        hold[...] = total
        for k, out in enumerate((o0, o1, o2, o3)):
            out[0, rows * i : rows * (i + 1)] = hold[lax.rem(here_ref[1] + k, 4)].astype(out.dtype)


def weight_grads(here, groups, ring):
    tokens, features = groups[0][0].shape
    columns = groups[0][2].shape[1]
    block = features // 16
    rows = block * len(groups)
    args = [a for group in groups for a in group]
    if ring:
        kernel, scratch = weight_grad_ring_kernel, [pltpu.VMEM((4, block, columns), F32)]
        outs = [shape((2, rows, columns), t) for t in (F32, BF, BF, BF)]
        out_specs = [pl.BlockSpec((1, rows, columns), lambda i, here: (i, 0, 0))] * 4
        first = 2
    else:
        kernel, scratch = weight_grad_kernel, []
        outs = [shape((4, 2, rows, columns), BF)]
        out_specs = [pl.BlockSpec((4, 1, rows, columns), lambda i, here: (0, i, 0, 0))]
        first = 3
    left = pl.BlockSpec(
        (tokens, features // 4), lambda i, here: (0, 2 * lax.rem(i + here[first], 2) + here[0])
    )
    right = pl.BlockSpec((tokens, columns), lambda i, here: (0, 0))
    return pl.pallas_call(
        kernel,
        grid_spec=pltpu.PrefetchScalarGridSpec(
            num_scalar_prefetch=1,
            grid=(2,),
            in_specs=[left, left, right, right] * len(groups),
            out_specs=out_specs,
            scratch_shapes=scratch,
        ),
        out_shape=outs,
        compiler_params=pltpu.CompilerParams(vmem_limit_bytes=56 * 2**20),
        cost_estimate=costs(2 * tokens * features * columns * len(groups), args),
    )(here, *args)


def near(array):
    return shifted(array, "core", 1)


def forward(x, weights, gains, tables, hook):
    w_in, w_out, w_feed = weights
    cos, sin, pos_here, pos_whole, unit_mask, here = tables
    x = x.astype(F32)
    normed = (x * norm_scale(x) * gains[0]).astype(BF)
    normed = gathered(normed, "z")
    tokens, features = normed.shape
    width = 4 * w_out[0].shape[1]
    units = w_feed.shape[1] - features
    queries, kv = call(
        qkv_kernel,
        [shape((tokens, width), BF), shape((tokens, 2 * width), BF)],
        2 * tokens * features * 3 * width,
        here, normed, cos, sin, halves=w_in,
    )
    kv = family(kv)
    mixed, lse, *parts = call(
        attend_kernel,
        [shape((tokens, width), BF), shape((tokens, width), F32), *part_shapes(features)],
        2 * tokens * width * (features + 8 * tokens),
        here, queries, kv, pos_here, pos_whole, halves=w_out,
    )
    parts[0] = hook(1, parts[0])
    middle = x + summed(parts, sent_home(parts))
    normed_two = (middle * norm_scale(middle) * gains[1]).astype(BF)
    normed_two = gathered(normed_two, "z")
    up = dot(normed_two, w_feed[:, :units])
    activated, slope = gelu_parts(up)
    activated = (activated * unit_mask).astype(BF)
    slope = slope * unit_mask
    parts = jnp.split(dot(activated, w_feed[:, units:]), 4, 0)
    parts[0] = hook(2, parts[0])
    received = sent_home([p.astype(BF) for p in parts])
    hidden = (middle + summed(parts, received)).astype(BF)
    lefts = [(a, near(a)) for a in (normed, mixed, normed_two, activated)]
    return hidden, (x, queries, kv, lse, middle, slope, lefts)


def norm_backward(v, grad_normed, gain, straight):
    scale = norm_scale(v)
    n = v * scale
    q = grad_normed * gain
    grad_gain = jnp.sum(grad_normed * n, 0)
    return straight + scale * (q - n * jnp.mean(q * n, -1, keepdims=True)), grad_gain


def backward(grad_out, kept, weights, gains, tables, hook, last):
    x, queries, kv, lse, middle, slope, lefts = kept
    normed, mixed, normed_two, activated = lefts
    w_in, w_out, w_feed = weights
    cos, sin, pos_here, pos_whole, unit_mask, here = tables
    tokens, width = queries.shape
    features = x.shape[1]
    units = slope.shape[1]
    branch = gathered(grad_out, "z")
    grad_out = grad_out.astype(F32)
    grad_up = (dot_t(branch, w_feed[:, units:]) * slope).astype(BF)
    parts = jnp.split(dot_t(grad_up, w_feed[:, :units]), 4, 0)
    received = sent_home([p.astype(BF) for p in parts])
    branch_near, grad_up_near = near(branch), near(grad_up)
    received = hook(1, received)
    grad_middle, grad_gain_two = norm_backward(middle, summed(parts, received), gains[1], grad_out)
    branch_low = grad_middle.astype(BF)
    groups = (
        (*normed_two, grad_up, grad_up_near),
        (*activated, branch, branch_near),
    )
    groups, branch_low = tied(groups, branch_low)
    ring = gather_ring(branch_low, "z")
    feed = weight_grads(here, groups, True)
    ring, feed = tied(ring, feed)
    ring = hook(2, ring, feed)
    branch = jnp.concatenate(ring, 0)
    dq, own, send, far = call(
        attend_back_kernel,
        [
            shape((tokens, width), BF),
            shape((tokens, 2 * width), F32),
            shape((2 * tokens, 2 * width), BF),
            shape((tokens, 2 * width), F32),
        ],
        2 * tokens * width * (features + 20 * tokens),
        here, branch, queries, kv, lse, pos_here, pos_whole, cos, sin, halves=w_out,
    )
    branch_near = near(branch)
    send = near(send)
    far = (far + send[tokens:].astype(F32)).astype(BF)
    far = shifted(far, "sec", 1)
    out = t_dot(jnp.concatenate(mixed, 0), jnp.concatenate([branch, branch_near], 0)).astype(BF)
    out = lax.dynamic_index_in_dim(out.reshape(2, 2, -1, features), here[0], 1, keepdims=False)
    far, out = tied(far, out)
    far = hook(3, far, out)
    grad_projected, *parts = call(
        project_back_kernel,
        [shape((tokens, 3 * width), BF), *part_shapes(features)],
        2 * tokens * width * 3 * features,
        here, dq, own, send[:tokens], far, cos, sin, halves=w_in,
    )
    received = sent_home(parts)
    g_in = weight_grads(here, [(*normed, grad_projected, near(grad_projected))], not last)
    received, g_in = tied(received, g_in)
    received = hook(4, received, g_in)
    grad_x, grad_gain_one = norm_backward(x, summed(parts, received), gains[0], grad_middle)
    return grad_x.astype(BF), (grad_gain_one, grad_gain_two)


def home_route():
    return [
        ((dp * 4 + y) * 4 + z, (y * 4 + z) * 4 + dp)
        for dp in range(4)
        for y in range(4)
        for z in range(4)
    ]


def local(
    inputs,
    cotangent,
    positions,
    granularity,
    attention_gain,
    attention_in,
    attention_out,
    feed_gain,
    feed_up,
    feed_down,
):
    sec = lax.axis_index("sec")
    rows, width_in = attention_in.shape[1:]
    model = attention_out.shape[2]
    units = feed_up.shape[2]

    core = lax.axis_index("core")
    x_0 = brought(inputs)

    def layered(mine):
        other = shifted(mine, "sec", 1)
        return jnp.where(sec == 0, mine, other), jnp.where(sec == 0, other, mine)

    def plane(block):
        each = jnp.broadcast_to(block[None], (8, *block.shape))
        mine = lax.all_to_all(each, ("xh", "y"), 0, 0, tiled=True)
        return mine.reshape(2, -1, block.shape[1])

    w_in = attention_in[0].reshape(rows, 3, 4, width_in // 12).transpose(2, 0, 1, 3)
    w_in = lax.all_to_all(w_in.reshape(4, rows, width_in // 4), "z", 0, 0, tiled=True)
    in_0, in_1 = layered(w_in.reshape(4 * rows, width_in // 4))
    gains = jnp.stack([attention_gain[0], feed_gain[0]])
    gains, in_0, in_1, w_up, w_out = tied(gains, in_0, in_1, feed_up[0], attention_out[0])
    in_0 = plane(in_0)
    gains = jnp.broadcast_to(gains[None], (128, 2, rows))
    gains = lax.all_to_all(gains, EVERY, 0, 0, tiled=True).reshape(2, 64, 2, rows)
    gains = gains.transpose(0, 2, 1, 3).reshape(2, 2, 64 * rows).astype(F32)
    w_up = w_up.reshape(rows, 16, 4, units // 64).transpose(2, 0, 1, 3)
    w_up = lax.all_to_all(w_up.reshape(4, rows, units // 4), "z", 0, 0, tiled=True)
    w_up = w_up.reshape(4 * rows, units // 4)
    w_out = lax.ppermute(w_out, ("xh", "core", "y", "z"), home_route())
    out_0, out_1 = layered(w_out)
    feed_0, feed_1 = layered(jnp.concatenate([w_up, feed_down[0]], 1))
    feed_0 = lax.all_gather(feed_0, PLANE, axis=0, tiled=True)
    feed_1 = lax.all_gather(feed_1, PLANE, axis=0, tiled=True)
    out_0 = plane(out_0)
    weights_0 = ((in_0, near(in_0)), (out_0, near(out_0)), feed_0)

    y = lax.axis_index("y")
    seq = lambda a: lax.dynamic_index_in_dim(a, y, 0, keepdims=False)
    facts = jnp.concatenate([positions, jnp.broadcast_to(granularity[:, None], (2, 128))], 1)
    other = shifted(facts, "core", 1)
    facts = jnp.where(core == 0, jnp.concatenate([facts, other]), jnp.concatenate([other, facts]))
    facts = seq(facts)
    level = facts[-1]
    pos = rolled(facts[:-128].reshape(2, 2, 4, -1), "z", 2)
    pos = rolled(rolled(pos, "core", 1), "sec", 0).reshape(4, -1)
    half = HEAD // 2
    freqs = jnp.exp(-math.log(THETA) * jnp.arange(half, dtype=F32) / half)
    angles = pos[0].astype(F32)[:, None] * freqs
    cos, sin = jnp.cos(angles), jnp.sin(angles)
    unit_width = (units // 32) * lax.shift_left(1, level)
    tables = (
        jnp.concatenate([cos, cos], 1),
        jnp.concatenate([-sin, sin], 1),
        pos[0][:, None],
        pos.reshape(1, -1),
        (jnp.arange(units // 4) < unit_width).astype(F32)[None],
        jnp.stack([core, y, lax.axis_index("xh"), 0]),
    )

    late = [in_1, out_1]

    def weights_hook(point, chain):
        chain, *late[:] = tied(chain, *late)
        if point == 1:
            late[:] = [plane(a) for a in late]
        return chain

    def no_hook(point, chain):
        return chain

    hidden_0, kept_0 = forward(x_0, weights_0, gains[0], tables, weights_hook)
    in_1, out_1 = late
    weights_1 = ((in_1, near(in_1)), (out_1, near(out_1)), feed_1)
    hidden_1, kept_1 = forward(hidden_0, weights_1, gains[1], tables, no_hook)

    def ring_sent(parts, ks):
        return [shifted(parts[k], "y", k) for k in ks]

    def ring_sum(parts, received):
        total = summed(parts, received)
        return total[0], shifted(total[1].astype(BF), "xh", 1)

    def met(block, home):
        return block.astype(F32), lax.ppermute(block.astype(BF), "sec", [(1 - home, home)])

    def total(pair):
        return pair[0] + pair[1].astype(F32)

    def columns_home(block):
        block = block.astype(BF).reshape(4, rows, -1)
        return lax.all_to_all(block, "z", 0, 0, tiled=True).astype(F32)

    def direct(out):
        out = out.reshape(8, rows, model)
        return lax.all_to_all(out, ("xh", "y"), 0, 0, tiled=True)

    at = {}

    def hold(chain, *names):
        values = [at[n] for n in names]
        chain, values = tied(chain, values)
        at.update(zip(names, values))
        return chain

    def hook_1(point, chain, *grads):
        if point == 1:
            at["hidden"] = returned(hidden_0, 0)
        if point == 2:
            at["feed"] = grads[0]
            at["a"] = ring_sent(grads[0], (1, 3))
            chain = hold(chain, "hidden")
        if point == 3:
            at["out"] = grads[0]
            chain = hold(chain, "feed")
            at["b"] = ring_sent(at["feed"], (2,))
        if point == 4:
            at["in"] = grads[0]
            chain = hold(chain, "a", "in", "out")
            at["c"] = ring_sent(at["in"], (1, 2, 3))
        return chain

    def hook_0(point, chain, *grads):
        if point == 1:
            chain = hold(chain, "b")
            at["feed"] = ring_sum(at["feed"], [*at["a"], *at["b"]])
            at["out"] = direct(at["out"])
        if point == 2:
            at["feed0"] = grads[0]
            at["a0"] = ring_sent(grads[0], (1, 3))
            chain = hold(chain, "c", "input_grad")
            at["in"] = ring_sum(at["in"], at["c"])
        if point == 3:
            at["out0"] = grads[0]
            chain = hold(chain, "feed", "feed0", "out")
            at["b0"] = ring_sent(at["feed0"], (2,))
            at["feed"] = met(total(at["feed"]), 1)
            at["out"] = met(jnp.sum(at["out"].astype(F32), 0), 1)
        if point == 4:
            at["in0"] = grads[0]
            chain = hold(chain, "in", "a0", "feed", "out", "in0")
            at["in"] = met(total(at["in"]), 1)
        return chain

    grad_1, gain_1 = backward(
        brought(cotangent), kept_1, weights_1, gains[1], tables, hook_1, False
    )
    at["input_grad"] = returned(grad_1, 1)
    grad_0, gain_0 = backward(grad_1, kept_0, weights_0, gains[0], tables, hook_0, True)
    hidden = jnp.where(sec == 0, at["hidden"], returned(hidden_1, 1))[None]
    input_grads = jnp.where(sec == 0, returned(grad_0, 0), at["input_grad"])[None]
    (in_0,) = at["in0"]
    in_0 = in_0.reshape(4, 2, 4, rows, -1).transpose(1, 0, 2, 3, 4).reshape(32, rows, -1)
    in_0 = lax.all_to_all(in_0, ("xh", "y", "z"), 0, 0, tiled=True).astype(F32)
    in_0 = total(met(jnp.sum(in_0.reshape(8, 4, rows, -1), 0), 0))
    feed_0 = total(met(total(ring_sum(at["feed0"], [*at["a0"], *at["b0"]])), 0))
    out_0 = total(met(jnp.sum(direct(at["out0"]).astype(F32), 0), 0))
    feed_1, in_1, out_1 = total(at["feed"]), total(at["in"]), total(at["out"])
    feed = jnp.where(sec == 0, feed_0, feed_1)
    g_up, g_down = jnp.split(feed, 2, 0)
    g_out = jnp.where(sec == 0, out_0, out_1)
    g_in = jnp.where(sec == 0, in_0, columns_home(in_1))
    g_in = g_in.reshape(4, rows, 3, width_in // 12).transpose(1, 2, 0, 3).reshape(rows, width_in)
    g_up = columns_home(g_up)
    g_up = g_up.reshape(4, rows, 16, units // 64).transpose(1, 2, 0, 3).reshape(rows, units)
    back = [(b, a) for a, b in home_route()]
    g_out = lax.ppermute(g_out.astype(BF), ("xh", "core", "y", "z"), back).astype(F32)

    gain_grads = jnp.stack([*gain_0, *gain_1]).reshape(2, 2, 64, rows).transpose(0, 2, 1, 3)
    gain_grads = gain_grads.reshape(128, 2, rows)
    gain_grads = jnp.sum(lax.all_to_all(gain_grads, EVERY, 0, 0, tiled=True), 0)
    return (
        hidden,
        input_grads,
        gain_grads[:1],
        g_in[None],
        g_out[None],
        gain_grads[1:],
        g_up[None],
        g_down[None],
    )


def solution(mesh):
    fine = Mesh(mesh.devices.reshape(2, 2, 2, 4, 4), EVERY)
    dp, ctx = ("xh", "core"), ("y", "z")
    ranks = dp + ctx
    in_specs = (
        P(dp, ctx, None),
        P(dp, ctx, None),
        P(dp, None),
        P(dp),
        P("sec", ranks),
        P("sec", ranks, None),
        P("sec", ranks, None),
        P("sec", ranks),
        P("sec", ranks, None),
        P("sec", ranks, None),
    )
    out_specs = (
        P("sec", dp, ctx, None),
        P("sec", dp, ctx, None),
        P("sec", ranks),
        P("sec", ranks, None),
        P("sec", ranks, None),
        P("sec", ranks),
        P("sec", ranks, None),
        P("sec", ranks, None),
    )
    return jax.shard_map(local, mesh=fine, in_specs=in_specs, out_specs=out_specs, check_vma=False)
```

```python
import math

import jax
import jax.numpy as jnp
from jax import lax
from jax.experimental import pallas as pl
from jax.experimental.pallas import tpu as pltpu
from jax.sharding import Mesh
from jax.sharding import PartitionSpec as P

HEAD = 128
EPS = 1e-05
THETA = 10000.0
MASKED = -1e30
BF = jnp.bfloat16
F32 = jnp.float32
PLANE = ("xh", "core", "y")
EVERY = ("sec", "xh", "core", "y", "z")


def shifted(block, axis, distance):
    n = lax.axis_size(axis)
    return lax.ppermute(block, axis, [(i, (i + distance) % n) for i in range(n)])


def gather_ring(block, axis):
    return [block] + [shifted(block, axis, k) for k in range(1, lax.axis_size(axis))]


def gathered(block, axis):
    return jnp.concatenate(gather_ring(block, axis), 0)


def scattered(blocks, axis):
    total = blocks[0].astype(F32)
    for k in range(1, lax.axis_size(axis)):
        total = total + shifted(blocks[k].astype(BF), axis, -k).astype(F32)
    return total


def rolled(array, axis_name, dim):
    n = lax.axis_size(axis_name)
    me = lax.axis_index(axis_name)
    return jnp.concatenate(
        [lax.dynamic_slice_in_dim(array, lax.rem(me - k + n, n), 1, dim) for k in range(n)], dim
    )


def family(block):
    near = shifted(block, "core", 1)
    far = shifted(block, "sec", 1)
    return jnp.concatenate([block, near, far, shifted(far, "core", 1)], 0)


def place(sec, core, y):
    return (sec * 2 + core) * 4 + y


def brought(pair):
    got = []
    for i in (0, 1):
        route = [
            (place(y // 2, core, y), place(y // 2, y % 2, 2 * core + i))
            for core in (0, 1)
            for y in range(4)
        ]
        got.append(lax.ppermute(pair[i], ("sec", "core", "y"), route))
    return jnp.where(lax.axis_index("y") % 2 == 0, got[0], got[1])


def returned(block, layer):
    got = []
    for i in (0, 1):
        route = [
            (place(sec, core, y), place(layer, y // 2, 2 * sec + core))
            for sec in (0, 1)
            for core in (0, 1)
            for y in (i, i + 2)
        ]
        got.append(lax.ppermute(block, ("sec", "core", "y"), route))
    return jnp.stack(got, -3)


def dot(a, b):
    return jnp.dot(a, b, preferred_element_type=F32)


def dot_t(a, b):
    return lax.dot_general(a, b, (((1,), (1,)), ((), ())), preferred_element_type=F32)


def t_dot(a, b):
    return lax.dot_general(a, b, (((0,), (0,)), ((), ())), preferred_element_type=F32)


def norm_scale(v):
    return lax.rsqrt(jnp.mean(v * v, -1, keepdims=True) + EPS)


def gelu_parts(up):
    phi = 0.5 + 0.5 * lax.erf(up * math.sqrt(0.5))
    density = jnp.exp(-0.5 * up * up) * (1.0 / math.sqrt(2.0 * math.pi))
    return up * phi, phi + up * density


def tied(*arrays):
    return lax.optimization_barrier(arrays)


VMEM = pl.BlockSpec(memory_space=pltpu.VMEM)
SMEM = pl.BlockSpec(memory_space=pltpu.SMEM)


LIGHT = pl.CostEstimate(flops=1, bytes_accessed=1, transcendentals=0)


def call(kernel, out_shape, here, *args, blocks=()):
    return pl.pallas_call(
        kernel,
        out_shape=out_shape,
        in_specs=[SMEM] + [VMEM] * len(args) + [pl.BlockSpec(memory_space=pl.ANY)] * len(blocks),
        out_specs=[VMEM] * len(out_shape),
        scratch_shapes=fetch_scratch(blocks) if blocks else [],
        compiler_params=pltpu.CompilerParams(vmem_limit_bytes=56 * 2**20),
        cost_estimate=LIGHT,
    )(here, *args, *blocks)


def shape(dims, dtype):
    return jax.ShapeDtypeStruct(dims, dtype)


def part_shapes(features):
    return [shape((64, features), F32)] + [shape((64, features), BF)] * 3


def store_parts(total, refs):
    for k, ref in enumerate(refs):
        ref[...] = total[64 * k : 64 * (k + 1)].astype(ref.dtype)


def summed(parts, received):
    total = parts[0].astype(F32)
    for r in received:
        total = total + r.astype(F32)
    return total


def sent_home(parts):
    return [shifted(parts[k], "z", -k) for k in range(1, 4)]


def swap_halves(v):
    return pltpu.roll(v, HEAD // 2, 1)


def fetches(here_ref, refs, whole, sems, lanes=slice(None)):
    copies = []
    each = len(refs) // 2
    ys = 4 if each > 1 or len(refs[0].shape) == 4 else 1
    for i, ref in enumerate(refs):
        core = here_ref[0] if i < each else 1 - here_ref[0]
        for j in range(ys // each):
            part = ref.at[j] if len(ref.shape) == 4 else ref
            y = j if each == 1 else lax.rem(here_ref[1] + 4 - i % each, 4)
            block = part.shape[1]
            for dx in (0, 1):
                xh = lax.rem(here_ref[2] + dx, 2)
                at = pl.multiple_of(((2 * xh + core) * ys + y) * block, 32)
                copy = pltpu.make_async_copy(
                    part.at[dx, :, lanes], whole.at[pl.ds(at, block), lanes], sems.at[len(copies)]
                )
                copy.start()
                copies.append(copy)
    return copies


def fetched(copies):
    for copy in copies:
        copy.wait()


def fetch_scratch(blocks):
    rows = sum(math.prod(a.shape[:-1]) for a in blocks)
    return [pltpu.VMEM((rows, blocks[0].shape[-1]), BF), pltpu.SemaphoreType.DMA((32,))]


def qkv_kernel(here_ref, n_ref, cos_ref, sin_ref, *refs):
    *refs, q_ref, kv_ref, whole, sems = refs
    fetched(fetches(here_ref, refs, whole, sems))
    width = q_ref.shape[1]
    cos, sin = cos_ref[...], sin_ref[...]
    for j in (0, 1, 2):
        ref, at = (q_ref, 0) if j == 0 else (kv_ref, (j - 1) * width)
        total = dot(n_ref[...], whole[:, j * width : (j + 1) * width])
        for h in range(0, width, HEAD):
            v = total[:, h : h + HEAD]
            if j < 2:
                v = v * cos + swap_halves(v) * sin
            ref[:, at + h : at + h + HEAD] = v.astype(BF)


def masked_scores(q, k, visible):
    return jnp.where(visible, dot_t(q, k) * (1.0 / math.sqrt(HEAD)), MASKED)


def attend_kernel(
    here_ref, q_ref, kv_ref, pq_ref, pk_ref, mine_ref, other_ref, mixed_ref, lse_ref, *refs
):
    *part_refs, whole, sems = refs
    copies = fetches(here_ref, (mine_ref, other_ref), whole, sems)
    width = q_ref.shape[1]
    visible = pk_ref[...] <= pq_ref[...]
    for i in range(width // HEAD):
        h = slice(i * HEAD, (i + 1) * HEAD)
        scores = masked_scores(q_ref[:, h], kv_ref[:, h], visible)
        most = jnp.max(scores, -1, keepdims=True)
        exponent = jnp.exp(scores - most)
        total = jnp.sum(exponent, -1, keepdims=True)
        probs = (exponent / total).astype(BF)
        values = kv_ref[:, width + i * HEAD : width + (i + 1) * HEAD]
        mixed_ref[:, h] = dot(probs, values).astype(BF)
        lse_ref[:, h] = jnp.broadcast_to(most + jnp.log(total), (q_ref.shape[0], HEAD))
    fetched(copies)
    store_parts(dot(mixed_ref[...], whole[...]), part_refs)


def attend_back_kernel(
    here_ref, b_ref, q_ref, kv_ref, lse_ref, pq_ref, pk_ref, cos_ref, sin_ref, mine_ref, other_ref,
    dq_ref, own_ref, send_ref, far_ref, whole, sems,
):
    fetched(fetches(here_ref, (mine_ref, other_ref), whole, sems))
    tokens, width = q_ref.shape
    scale = 1.0 / math.sqrt(HEAD)
    visible = pk_ref[...] <= pq_ref[...]
    grad_mixed = dot_t(b_ref[...], whole[...]).astype(BF)
    for i in range(width // HEAD):
        h = slice(i * HEAD, (i + 1) * HEAD)
        vh = slice(width + i * HEAD, width + (i + 1) * HEAD)
        q, k, v, g = q_ref[:, h], kv_ref[:, h], kv_ref[:, vh], grad_mixed[:, h]
        probs = jnp.exp(masked_scores(q, k, visible) - lse_ref[:, i * HEAD : i * HEAD + 1])
        grad_probs = dot_t(g, v)
        weighted = jnp.sum(probs * grad_probs, -1, keepdims=True)
        grad_scores = (probs * (grad_probs - weighted)).astype(BF)
        dq = dot(grad_scores, k) * scale
        dq_ref[:, h] = (dq * cos_ref[...] - swap_halves(dq) * sin_ref[...]).astype(BF)
        for lanes, grad in (
            (h, t_dot(grad_scores, q) * scale),
            (vh, t_dot(probs.astype(BF), g)),
        ):
            own_ref[:, lanes] = grad[:tokens]
            send_ref[:tokens, lanes] = grad[tokens : 2 * tokens].astype(BF)
            far_ref[:, lanes] = grad[2 * tokens : 3 * tokens]
            send_ref[tokens:, lanes] = grad[3 * tokens :].astype(BF)


def project_back_kernel(here_ref, dq_ref, own_ref, near_ref, far_ref, cos_ref, sin_ref, *refs):
    *refs, grad_ref, p0, p1, p2, p3, whole, sems = refs
    part_refs = (p0, p1, p2, p3)
    copies = fetches(here_ref, refs, whole, sems)
    width = dq_ref.shape[1]
    grad_ref[:, :width] = dq_ref[...]
    for h in range(0, 2 * width, HEAD):
        lanes = slice(h, h + HEAD)
        near = near_ref[: dq_ref.shape[0], lanes]
        v = own_ref[:, lanes] + near.astype(F32) + far_ref[:, lanes].astype(F32)
        if h < width:
            v = v * cos_ref[...] - swap_halves(v) * sin_ref[...]
        grad_ref[:, width + h : width + h + HEAD] = v.astype(BF)
    fetched(copies)
    store_parts(dot_t(grad_ref[...], whole[...]), part_refs)


def feed_kernel(here_ref, n_ref, mask_ref, mine_ref, other_ref, act_ref, slope_ref, *refs):
    *part_refs, whole, sems = refs
    units = act_ref.shape[1]
    pair = (mine_ref, other_ref)
    ups = fetches(here_ref, pair, whole, sems.at[pl.ds(0, 16)], slice(0, units))
    downs = fetches(here_ref, pair, whole, sems.at[pl.ds(16, 16)], slice(units, None))
    fetched(ups)
    step = units // 4
    for at in range(0, units, step):
        lanes = slice(at, at + step)
        value, slope = gelu_parts(dot(n_ref[...], whole[:, lanes]))
        act_ref[:, lanes] = (value * mask_ref[:, lanes]).astype(BF)
        slope_ref[:, lanes] = slope * mask_ref[:, lanes]
    fetched(downs)
    store_parts(dot(act_ref[...], whole[:, units:]), part_refs)


def feed_back_kernel(here_ref, b_ref, slope_ref, mine_ref, other_ref, grad_ref, *refs):
    *part_refs, whole, sems = refs
    units = grad_ref.shape[1]
    pair = (mine_ref, other_ref)
    downs = fetches(here_ref, pair, whole, sems.at[pl.ds(16, 16)], slice(units, None))
    ups = fetches(here_ref, pair, whole, sems.at[pl.ds(0, 16)], slice(0, units))
    fetched(downs)
    grad_ref[...] = (dot_t(b_ref[...], whole[:, units:]) * slope_ref[...]).astype(BF)
    fetched(ups)
    store_parts(dot_t(grad_ref[...], whole[:, :units]), part_refs)


def block_grads(refs):
    for i in range(len(refs) // 4):
        left, left_near, right, right_near = refs[4 * i : 4 * i + 4]
        total = t_dot(left[...], right[...]) + t_dot(left_near[...], right_near[...])
        yield i, total.reshape(4, total.shape[0] // 4, total.shape[1])


def weight_grad_kernel(here_ref, *refs):
    *refs, out_ref = refs
    for i, total in block_grads(refs):
        rows = total.shape[1]
        out_ref[:, 0, rows * i : rows * (i + 1)] = total.astype(BF)


def weight_grads(here, groups):
    tokens, features = groups[0][0].shape
    columns = groups[0][2].shape[1]
    rows = features // 16 * len(groups)
    args = [a for group in groups for a in group]
    left = pl.BlockSpec((tokens, features // 4), lambda i, here: (0, 2 * i + here[0]))
    right = pl.BlockSpec((tokens, columns), lambda i, here: (0, 0))
    return pl.pallas_call(
        weight_grad_kernel,
        grid_spec=pltpu.PrefetchScalarGridSpec(
            num_scalar_prefetch=1,
            grid=(2,),
            in_specs=[left, left, right, right] * len(groups),
            out_specs=pl.BlockSpec((4, 1, rows, columns), lambda i, here: (0, i, 0, 0)),
        ),
        out_shape=shape((4, 2, rows, columns), BF),
        compiler_params=pltpu.CompilerParams(vmem_limit_bytes=56 * 2**20),
        cost_estimate=LIGHT,
    )(here, *args)


def near(array):
    return shifted(array, "core", 1)


def with_near(arrays):
    return [*arrays, *(near(a) for a in arrays)]


def layer_pairs(shard):
    sec = lax.axis_index("sec")
    places = [(sec, xh) for sec in (0, 1) for xh in (0, 1)]
    across = [(2 * s + x, 2 * (1 - s) + 1 - x) for s, x in places]
    own = jnp.stack([shard, shifted(shard, "xh", 1)])
    other = jnp.stack([shifted(shard, "sec", 1), lax.ppermute(shard, ("sec", "xh"), across)])
    return jnp.where(sec == 0, own, other), jnp.where(sec == 0, other, own)


def y_gathered(pair):
    return lax.all_gather(pair, "y", axis=0, tiled=False)


def scaled(v):
    return (v * norm_scale(v)).astype(BF)


def attention(x, normed, w_out, tables, hook):
    cos, sin, pos_here, pos_whole, unit_mask, here = tables
    x = x.astype(F32)
    w_in, normed = hook(0, normed)
    normed = jnp.concatenate(normed, 0)
    tokens, features = normed.shape
    width = w_in[0].shape[-1] // 3
    queries, kv = call(
        qkv_kernel,
        [shape((tokens, width), BF), shape((tokens, 2 * width), BF)],
        here, normed, cos, sin, blocks=w_in,
    )
    kv = hook(1, kv)
    kv = family(kv)
    kv = hook(2, kv)
    mixed, lse, *parts = call(
        attend_kernel,
        [shape((tokens, width), BF), shape((tokens, width), F32), *part_shapes(features)],
        here, queries, kv, pos_here, pos_whole, blocks=w_out(),
    )
    parts[0] = hook(3, parts[0])
    middle = x + summed(parts, sent_home(parts))
    return middle, (x, queries, kv, lse, middle), [(a, near(a)) for a in (normed, mixed)], w_in


def feed_forward(middle, w_feed, tables, hook):
    features = middle.shape[1]
    mask, here = tables[4:]
    tokens, units = 4 * middle.shape[0], mask.shape[1]
    normed = gathered(scaled(middle), "z")
    normed = hook(4, normed)
    activated, slope, *parts = call(
        feed_kernel,
        [shape((tokens, units), BF), shape((tokens, units), F32), *part_shapes(features)],
        here, normed, mask, blocks=w_feed(),
    )
    parts[0] = hook(5, parts[0])
    return parts, slope, [(a, near(a)) for a in (normed, activated)]


def arrived(middle, parts, received):
    return (middle + summed(parts, received)).astype(BF)


def norm_backward(v, q, straight):
    scale = norm_scale(v)
    n = v * scale
    return straight + scale * (q - n * jnp.mean(q * n, -1, keepdims=True))


def backward(grad_out, branch, kept, slope, lefts, weights, tables, hook):
    x, queries, kv, lse, middle = kept
    normed, mixed, normed_two, activated = lefts
    w_in, w_out, w_feed = weights
    cos, sin, pos_here, pos_whole, unit_mask, here = tables
    tokens, width = queries.shape
    features = x.shape[1]
    units = slope.shape[1]
    branch = jnp.concatenate(hook(0, branch), 0)
    grad_out = grad_out.astype(F32)
    grad_up, *parts = call(
        feed_back_kernel,
        [shape((tokens, units), BF), *part_shapes(features)],
        here, branch, slope, blocks=w_feed,
    )
    received = sent_home(parts)
    branch_near, grad_up_near = near(branch), near(grad_up)
    received = hook(1, received)
    grad_middle = norm_backward(middle, summed(parts, received), grad_out)
    branch_low = grad_middle.astype(BF)
    groups = (
        (*normed_two, grad_up, grad_up_near),
        (*activated, branch, branch_near),
    )
    groups, branch_low = tied(groups, branch_low)
    ring = gather_ring(branch_low, "z")
    feed = weight_grads(here, groups)
    ring, feed = tied(ring, feed)
    ring = hook(2, ring, feed)
    branch = jnp.concatenate(ring, 0)
    dq, own, send, far = call(
        attend_back_kernel,
        [
            shape((tokens, width), BF),
            shape((tokens, 2 * width), F32),
            shape((2 * tokens, 2 * width), BF),
            shape((tokens, 2 * width), F32),
        ],
        here, branch, queries, kv, lse, pos_here, pos_whole, cos, sin, blocks=w_out,
    )
    dq, own, send, far = hook(6, (dq, own, send, far))
    branch_near = near(branch)
    send = near(send)
    far = (far + send[tokens:].astype(F32)).astype(BF)
    far = shifted(far, "sec", 1)
    out = t_dot(jnp.concatenate(mixed, 0), jnp.concatenate([branch, branch_near], 0)).astype(BF)
    out = lax.dynamic_index_in_dim(out.reshape(2, 2, -1, features), here[0], 1, keepdims=False)
    out = out.reshape(2, 4, -1, features).transpose(1, 0, 2, 3)
    far, out = tied(far, out)
    far = hook(3, far, out)
    grad_projected, *parts = call(
        project_back_kernel,
        [shape((tokens, 3 * width), BF), *part_shapes(features)],
        here, dq, own, send, far, cos, sin, blocks=w_in,
    )
    parts = hook(5, parts)
    received = sent_home(parts)
    g_in = weight_grads(here, [(*normed, grad_projected, near(grad_projected))])
    received, g_in = tied(received, g_in)
    received = hook(4, received, g_in)
    return norm_backward(x, summed(parts, received), grad_middle).astype(BF)


def home_route():
    return [
        ((dp * 4 + y) * 4 + z, (y * 4 + z) * 4 + dp)
        for dp in range(4)
        for y in range(4)
        for z in range(4)
    ]


def local(
    inputs,
    cotangent,
    positions,
    granularity,
    attention_gain,
    attention_in,
    attention_out,
    feed_gain,
    feed_up,
    feed_down,
):
    sec = lax.axis_index("sec")
    rows, width_in = attention_in.shape[1:]
    model = attention_out.shape[2]
    units = feed_up.shape[2]

    core = lax.axis_index("core")

    def layered(mine):
        other = shifted(mine, "sec", 1)
        return jnp.where(sec == 0, mine, other), jnp.where(sec == 0, other, mine)

    def with_gain(weight, gain):
        return (weight.astype(F32) * gain.astype(F32)[:, None]).astype(BF)

    w_in = with_gain(attention_in[0], attention_gain[0])
    w_up = with_gain(feed_up[0], feed_gain[0])
    w_in = w_in.reshape(rows, 3, 4, width_in // 12).transpose(2, 0, 1, 3)
    w_up = w_up.reshape(rows, 16, 4, units // 64).transpose(2, 0, 1, 3)
    both = [w_in.reshape(4, rows, width_in // 4), w_up.reshape(4, rows, units // 4)]
    both = lax.all_to_all(jnp.concatenate(both, 2), "z", 0, 0, tiled=True)
    outs = lax.ppermute(attention_out[0], ("xh", "core", "y", "z"), home_route())
    both, inputs, positions, outs = tied(both.reshape(4 * rows, -1), inputs, positions, outs)
    in_0, in_1 = layer_pairs(both[:, : width_in // 4])
    outs = jnp.stack(layer_pairs(outs))
    feed = jnp.concatenate([both[:, width_in // 4 :], feed_down[0]], 1)
    x_0 = brought(inputs)
    feed, in_0, in_1, outs, x_0 = tied(feed, in_0, in_1, outs, x_0)
    in_0 = gather_ring(in_0, "y")
    outs = y_gathered(outs).transpose(1, 2, 0, 3, 4).reshape(2, 2, 4 * rows, model)
    feed_0, feed_1 = layer_pairs(feed)
    normed_0 = gather_ring(scaled(x_0.astype(F32)), "z")
    in_0, feed_0, feed_1, normed_0 = tied(in_0, feed_0, feed_1, normed_0)
    feed_0 = y_gathered(feed_0)
    outs = [with_near([a]) for a in outs]

    y = lax.axis_index("y")
    seq = lambda a: lax.dynamic_index_in_dim(a, y, 0, keepdims=False)
    facts = jnp.concatenate([positions, jnp.broadcast_to(granularity[:, None], (2, 128))], 1)
    other = shifted(facts, "core", 1)
    facts = jnp.where(core == 0, jnp.concatenate([facts, other]), jnp.concatenate([other, facts]))
    facts = seq(facts)
    level = facts[-1]
    pos = rolled(facts[:-128].reshape(2, 2, 4, -1), "z", 2)
    pos = rolled(rolled(pos, "core", 1), "sec", 0).reshape(4, -1)
    here = jnp.stack([core, y, lax.axis_index("xh"), 0])
    half = HEAD // 2
    freqs = jnp.exp(-math.log(THETA) * jnp.arange(half, dtype=F32) / half)
    angles = pos[0].astype(F32)[:, None] * freqs
    cos, sin = jnp.cos(angles), jnp.sin(angles)
    unit_width = (units // 32) * lax.shift_left(1, level)
    tables = (
        jnp.concatenate([cos, cos], 1),
        jnp.concatenate([-sin, sin], 1),
        pos[0][:, None],
        pos.reshape(1, -1),
        (jnp.arange(units // 4) < unit_width).astype(F32)[None],
        here,
    )

    at = {"in_0": in_0, "in": in_1, "feed": feed_1, "cotangent": cotangent, "feed_0": feed_0}
    at["outs"] = outs

    def hold(chain, *names):
        values = [at[n] for n in names]
        chain, values = tied(chain, values)
        at.update(zip(names, values))
        return chain

    def forward_0(point, chain, *more):
        if point == 0:
            chain = hold(chain, "in_0")
            return with_near(at["in_0"]), chain
        if point == 1:
            chain = hold(chain, "outs")
        if point == 2:
            chain = hold(chain, "in", "feed")
            at["in"], at["feed"] = y_gathered(at["in"]), y_gathered(at["feed"])
        if point == 3:
            chain = hold(chain, "cotangent", "feed_0")
            at["feed_0"] = with_near([at["feed_0"]])
            at["cotangent"] = brought(at["cotangent"])
        if point == 5:
            chain = hold(chain, "in", "cotangent")
            at["in"] = with_near([at["in"]])
        return chain

    def forward_1(point, chain, *more):
        if point == 0:
            chain = hold(chain, "in")
            return at["in"], chain
        if point == 1:
            at["branch"] = gather_ring(at["cotangent"], "z")
        if point == 3:
            chain = hold(chain, "branch", "feed")
            at["feed"] = with_near([at["feed"]])
        return chain

    middle_0, kept_0, lefts_0, in_0 = attention(
        x_0, normed_0, lambda: at["outs"][0], tables, forward_0
    )
    parts, slope_0, more = feed_forward(middle_0, lambda: at["feed_0"], tables, forward_0)
    lefts_0 += more
    hidden_0 = arrived(middle_0, parts, sent_home(parts))
    middle_1, kept_1, lefts_1, in_1 = attention(
        hidden_0, gather_ring(scaled(hidden_0.astype(F32)), "z"), lambda: at["outs"][1], tables, forward_1
    )
    parts_1, slope_1, more = feed_forward(middle_1, lambda: at["feed"], tables, forward_1)
    lefts_1 += more
    feed_0, feed_1, cotangent = at["feed_0"], at["feed"], at["cotangent"]
    out_0, out_1 = at["outs"]

    def y_sum(grads):
        flat = grads.reshape(-1, grads.shape[-1])
        flat = lax.psum_scatter(flat, "y", scatter_dimension=0, tiled=True)
        return flat.reshape(grads.shape[1:])

    def x_sum(zero, one):
        both = jnp.concatenate([zero, one], 0)
        both = lax.all_to_all(both, ("sec", "xh"), 0, 0, tiled=True)
        return jnp.sum(both.astype(F32), 0)

    at["parts"] = parts_1

    def backward_1(point, chain, *grads):
        if point == 2:
            at["feed1"] = y_sum(grads[0])
            chain = hold(chain, "parts")
            at["received"] = sent_home(at["parts"])
        if point == 6:
            chain = hold(chain, "received")
        if point == 3:
            at["out1"] = y_sum(grads[0])
        if point == 4:
            chain = hold(chain, "feed1")
            at["in1"] = y_sum(grads[0])
        return chain

    def attention_pair(grad_in, out):
        return jnp.concatenate([grad_in, out.reshape(2, -1, width_in // 4)], 1)

    def backward_0(point, chain, *grads):
        if point == 2:
            chain = hold(chain, "out1", "in1")
            at["feed0"] = y_sum(grads[0])
        if point == 3:
            at["out0"] = y_sum(grads[0])
        if point == 5:
            chain = hold(chain, "feed0")
            at["up"], at["down"] = (
                x_sum(at["feed0"][:, a : a + 4 * rows], at["feed1"][:, a : a + 4 * rows])
                for a in (0, 4 * rows)
            )
        if point == 4:
            at["in0"] = y_sum(grads[0])
        return chain

    grad_1 = backward(
        cotangent, at["branch"], kept_1, slope_1, lefts_1,
        (in_1, out_1, feed_1), tables, backward_1,
    )
    at["to_1"] = jnp.stack([arrived(middle_1, at["parts"], at["received"]), grad_1])
    grad_0 = backward(
        grad_1, gather_ring(grad_1, "z"), kept_0, slope_0, lefts_0,
        (in_0, out_0, feed_0), tables, backward_0,
    )
    def columns_home(block):
        block = block.astype(BF).reshape(4, rows, -1)
        return lax.all_to_all(block, "z", 0, 0, tiled=True).astype(F32)

    to_0, to_1 = returned(jnp.stack([hidden_0, grad_0]), 0), returned(at["to_1"], 1)
    hidden, input_grads = (jnp.where(sec == 0, a, b)[None] for a, b in zip(to_0, to_1))
    g_up, g_down = columns_home(at["up"]), at["down"]
    attn = x_sum(attention_pair(at["in0"], at["out0"]), attention_pair(at["in1"], at["out1"]))
    g_in, g_out = columns_home(attn[: 4 * rows]), attn[4 * rows :].reshape(rows, model)
    g_in = g_in.reshape(4, rows, 3, width_in // 12).transpose(1, 2, 0, 3).reshape(rows, width_in)
    g_up = g_up.reshape(4, rows, 16, units // 64).transpose(1, 2, 0, 3).reshape(rows, units)
    back = [(b, a) for a, b in home_route()]
    g_out = lax.ppermute(g_out.astype(BF), ("xh", "core", "y", "z"), back).astype(F32)


    def home(grad, weight, gain):
        return grad * gain.astype(F32)[:, None], jnp.sum(grad * weight.astype(F32), 1)

    g_in, g_gain = home(g_in, attention_in[0], attention_gain[0])
    g_up, g_gain_two = home(g_up, feed_up[0], feed_gain[0])
    return (
        hidden,
        input_grads,
        g_gain[None],
        g_in[None],
        g_out[None],
        g_gain_two[None],
        g_up[None],
        g_down[None],
    )


def solution(mesh):
    fine = Mesh(mesh.devices.reshape(2, 2, 2, 4, 4), EVERY)
    dp, ctx = ("xh", "core"), ("y", "z")
    ranks = dp + ctx
    in_specs = (
        P(dp, ctx, None),
        P(dp, ctx, None),
        P(dp, None),
        P(dp),
        P("sec", ranks),
        P("sec", ranks, None),
        P("sec", ranks, None),
        P("sec", ranks),
        P("sec", ranks, None),
        P("sec", ranks, None),
    )
    out_specs = (
        P("sec", dp, ctx, None),
        P("sec", dp, ctx, None),
        P("sec", ranks),
        P("sec", ranks, None),
        P("sec", ranks, None),
        P("sec", ranks),
        P("sec", ranks, None),
        P("sec", ranks, None),
    )
    return jax.shard_map(local, mesh=fine, in_specs=in_specs, out_specs=out_specs, check_vma=False)
```

```python
import math

import jax
import jax.numpy as jnp
from jax import lax
from jax.experimental import pallas as pl
from jax.experimental.pallas import tpu as pltpu
from jax.sharding import Mesh
from jax.sharding import PartitionSpec as P

HEAD = 128
EPS = 1e-05
THETA = 10000.0
MASKED = -1e30
BF = jnp.bfloat16
F32 = jnp.float32
PLANE = ("xh", "core", "y")
EVERY = ("sec", "xh", "core", "y", "z")


def shifted(block, axis, distance):
    n = lax.axis_size(axis)
    return lax.ppermute(block, axis, [(i, (i + distance) % n) for i in range(n)])


def gather_ring(block, axis):
    return [block] + [shifted(block, axis, k) for k in range(1, lax.axis_size(axis))]


def gathered(block, axis):
    return jnp.concatenate(gather_ring(block, axis), 0)


def scattered(blocks, axis):
    total = blocks[0].astype(F32)
    for k in range(1, lax.axis_size(axis)):
        total = total + shifted(blocks[k].astype(BF), axis, -k).astype(F32)
    return total


def rolled(array, axis_name, dim):
    n = lax.axis_size(axis_name)
    me = lax.axis_index(axis_name)
    return jnp.concatenate(
        [lax.dynamic_slice_in_dim(array, lax.rem(me - k + n, n), 1, dim) for k in range(n)], dim
    )


def family(block):
    near = shifted(block, "core", 1)
    far = shifted(block, "sec", 1)
    return jnp.concatenate([block, near, far, shifted(far, "core", 1)], 0)


def place(sec, core, y):
    return (sec * 2 + core) * 4 + y


def brought(pair):
    got = []
    for i in (0, 1):
        route = [
            (place(y // 2, core, y), place(y // 2, y % 2, 2 * core + i))
            for core in (0, 1)
            for y in range(4)
        ]
        got.append(lax.ppermute(pair[i], ("sec", "core", "y"), route))
    return jnp.where(lax.axis_index("y") % 2 == 0, got[0], got[1])


def returned(block, layer):
    got = []
    for i in (0, 1):
        route = [
            (place(sec, core, y), place(layer, y // 2, 2 * sec + core))
            for sec in (0, 1)
            for core in (0, 1)
            for y in (i, i + 2)
        ]
        got.append(lax.ppermute(block, ("sec", "core", "y"), route))
    return jnp.stack(got, -3)


def dot(a, b):
    return jnp.dot(a, b, preferred_element_type=F32)


def dot_t(a, b):
    return lax.dot_general(a, b, (((1,), (1,)), ((), ())), preferred_element_type=F32)


def t_dot(a, b):
    return lax.dot_general(a, b, (((0,), (0,)), ((), ())), preferred_element_type=F32)


def norm_scale(v):
    return lax.rsqrt(jnp.mean(v * v, -1, keepdims=True) + EPS)


def gelu_parts(up):
    phi = 0.5 + 0.5 * lax.erf(up * math.sqrt(0.5))
    density = jnp.exp(-0.5 * up * up) * (1.0 / math.sqrt(2.0 * math.pi))
    return up * phi, phi + up * density


def tied(*arrays):
    return lax.optimization_barrier(arrays)


VMEM = pl.BlockSpec(memory_space=pltpu.VMEM)
SMEM = pl.BlockSpec(memory_space=pltpu.SMEM)


LIGHT = pl.CostEstimate(flops=1, bytes_accessed=1, transcendentals=0)


def call(kernel, out_shape, here, *args, rows, blocks):
    return pl.pallas_call(
        kernel,
        out_shape=out_shape,
        in_specs=[SMEM] + [VMEM] * len(args) + [pl.BlockSpec(memory_space=pl.ANY)] * len(blocks),
        out_specs=[VMEM] * len(out_shape),
        scratch_shapes=fetch_scratch(rows, blocks),
        compiler_params=pltpu.CompilerParams(vmem_limit_bytes=56 * 2**20),
        cost_estimate=LIGHT,
    )(here, *args, *blocks)


def shape(dims, dtype):
    return jax.ShapeDtypeStruct(dims, dtype)


def part_shapes(features):
    return [shape((64, features), F32)] + [shape((64, features), BF)] * 3


def store_parts(total, refs):
    for k, ref in enumerate(refs):
        ref[...] = total[64 * k : 64 * (k + 1)].astype(ref.dtype)


def summed(parts, received):
    total = parts[0].astype(F32)
    for r in received:
        total = total + r.astype(F32)
    return total


def sent_home(parts):
    return [shifted(parts[k], "z", -k) for k in range(1, 4)]


def swap_halves(v):
    return pltpu.roll(v, HEAD // 2, 1)


def fetches(here_ref, refs, whole, sems, lanes=slice(None)):
    copies = []
    each = len(refs) // 2
    ys = 4 if each > 1 or len(refs[0].shape) == 4 else 1
    for i, ref in enumerate(refs):
        core = here_ref[0] if i < each else 1 - here_ref[0]
        for j in range(ys // each):
            part = ref.at[j] if len(ref.shape) == 4 else ref
            y = j if each == 1 else lax.rem(here_ref[1] + 4 - i % each, 4)
            block = whole.shape[0] // (4 * ys)
            for dx in (0, 1):
                xh = lax.rem(here_ref[2] + dx, 2)
                at = pl.multiple_of(((2 * xh + core) * ys + y) * block, 32)
                copy = pltpu.make_async_copy(
                    part.at[dx, pl.ds(0, block), lanes],
                    whole.at[pl.ds(at, block), lanes],
                    sems.at[len(copies)],
                )
                copy.start()
                copies.append(copy)
    return copies


def fetched(copies):
    for copy in copies:
        copy.wait()


def fetch_scratch(rows, blocks):
    return [pltpu.VMEM((rows, blocks[0].shape[-1]), BF), pltpu.SemaphoreType.DMA((32,))]


def qkv_kernel(here_ref, n_ref, cos_ref, sin_ref, *refs):
    *refs, q_ref, kv_ref, whole, sems = refs
    fetched(fetches(here_ref, refs, whole, sems))
    width = q_ref.shape[1]
    cos, sin = cos_ref[...], sin_ref[...]
    for j in (0, 1, 2):
        ref, at = (q_ref, 0) if j == 0 else (kv_ref, (j - 1) * width)
        total = dot(n_ref[...], whole[:, j * width : (j + 1) * width])
        for h in range(0, width, HEAD):
            v = total[:, h : h + HEAD]
            if j < 2:
                v = v * cos + swap_halves(v) * sin
            ref[:, at + h : at + h + HEAD] = v.astype(BF)


def masked_scores(q, k, visible):
    return jnp.where(visible, dot_t(q, k) * (1.0 / math.sqrt(HEAD)), MASKED)


def attend_kernel(
    here_ref, q_ref, kv_ref, pq_ref, pk_ref, mine_ref, other_ref, mixed_ref, lse_ref, *refs
):
    *part_refs, whole, sems = refs
    copies = fetches(here_ref, (mine_ref, other_ref), whole, sems)
    width = q_ref.shape[1]
    visible = pk_ref[...] <= pq_ref[...]
    for i in range(width // HEAD):
        h = slice(i * HEAD, (i + 1) * HEAD)
        scores = masked_scores(q_ref[:, h], kv_ref[:, h], visible)
        most = jnp.max(scores, -1, keepdims=True)
        exponent = jnp.exp(scores - most)
        total = jnp.sum(exponent, -1, keepdims=True)
        probs = (exponent / total).astype(BF)
        values = kv_ref[:, width + i * HEAD : width + (i + 1) * HEAD]
        mixed_ref[:, h] = dot(probs, values).astype(BF)
        lse_ref[:, h] = jnp.broadcast_to(most + jnp.log(total), (q_ref.shape[0], HEAD))
    fetched(copies)
    store_parts(dot(mixed_ref[...], whole[...]), part_refs)


def attend_back_kernel(
    here_ref, b_ref, q_ref, kv_ref, lse_ref, pq_ref, pk_ref, cos_ref, sin_ref, mine_ref, other_ref,
    dq_ref, own_ref, send_ref, far_ref, whole, sems,
):
    fetched(fetches(here_ref, (mine_ref, other_ref), whole, sems))
    tokens, width = q_ref.shape
    scale = 1.0 / math.sqrt(HEAD)
    visible = pk_ref[...] <= pq_ref[...]
    grad_mixed = dot_t(b_ref[...], whole[...]).astype(BF)
    for i in range(width // HEAD):
        h = slice(i * HEAD, (i + 1) * HEAD)
        vh = slice(width + i * HEAD, width + (i + 1) * HEAD)
        q, k, v, g = q_ref[:, h], kv_ref[:, h], kv_ref[:, vh], grad_mixed[:, h]
        probs = jnp.exp(masked_scores(q, k, visible) - lse_ref[:, i * HEAD : i * HEAD + 1])
        grad_probs = dot_t(g, v)
        weighted = jnp.sum(probs * grad_probs, -1, keepdims=True)
        grad_scores = (probs * (grad_probs - weighted)).astype(BF)
        dq = dot(grad_scores, k) * scale
        dq_ref[:, h] = (dq * cos_ref[...] - swap_halves(dq) * sin_ref[...]).astype(BF)
        for lanes, grad in (
            (h, t_dot(grad_scores, q) * scale),
            (vh, t_dot(probs.astype(BF), g)),
        ):
            own_ref[:, lanes] = grad[:tokens]
            send_ref[:tokens, lanes] = grad[tokens : 2 * tokens].astype(BF)
            far_ref[:, lanes] = grad[2 * tokens : 3 * tokens]
            send_ref[tokens:, lanes] = grad[3 * tokens :].astype(BF)


def project_back_kernel(here_ref, dq_ref, own_ref, near_ref, far_ref, cos_ref, sin_ref, *refs):
    *refs, grad_ref, p0, p1, p2, p3, whole, sems = refs
    part_refs = (p0, p1, p2, p3)
    copies = fetches(here_ref, refs, whole, sems)
    width = dq_ref.shape[1]
    grad_ref[:, :width] = dq_ref[...]
    for h in range(0, 2 * width, HEAD):
        lanes = slice(h, h + HEAD)
        near = near_ref[: dq_ref.shape[0], lanes]
        v = own_ref[:, lanes] + near.astype(F32) + far_ref[:, lanes].astype(F32)
        if h < width:
            v = v * cos_ref[...] - swap_halves(v) * sin_ref[...]
        grad_ref[:, width + h : width + h + HEAD] = v.astype(BF)
    fetched(copies)
    store_parts(dot_t(grad_ref[...], whole[...]), part_refs)


def feed_kernel(here_ref, n_ref, mask_ref, mine_ref, other_ref, act_ref, slope_ref, *refs):
    *part_refs, whole, sems = refs
    units = act_ref.shape[1]
    pair = (mine_ref, other_ref)
    ups = fetches(here_ref, pair, whole, sems.at[pl.ds(0, 16)], slice(0, units))
    downs = fetches(here_ref, pair, whole, sems.at[pl.ds(16, 16)], slice(units, None))
    fetched(ups)
    step = units // 4
    for at in range(0, units, step):
        lanes = slice(at, at + step)
        value, slope = gelu_parts(dot(n_ref[...], whole[:, lanes]))
        act_ref[:, lanes] = (value * mask_ref[:, lanes]).astype(BF)
        slope_ref[:, lanes] = slope * mask_ref[:, lanes]
    fetched(downs)
    store_parts(dot(act_ref[...], whole[:, units:]), part_refs)


def feed_back_kernel(here_ref, b_ref, slope_ref, mine_ref, other_ref, grad_ref, *refs):
    *part_refs, whole, sems = refs
    units = grad_ref.shape[1]
    pair = (mine_ref, other_ref)
    downs = fetches(here_ref, pair, whole, sems.at[pl.ds(16, 16)], slice(units, None))
    ups = fetches(here_ref, pair, whole, sems.at[pl.ds(0, 16)], slice(0, units))
    fetched(downs)
    grad_ref[...] = (dot_t(b_ref[...], whole[:, units:]) * slope_ref[...]).astype(BF)
    fetched(ups)
    store_parts(dot_t(grad_ref[...], whole[:, :units]), part_refs)


def feed_both_kernel(here_ref, n_ref, mask_ref, b_ref, mine_ref, other_ref, act_ref, grad_ref, *refs):
    *part_refs, whole, sems = refs
    units = act_ref.shape[1]
    pair = (mine_ref, other_ref)
    ups = fetches(here_ref, pair, whole, sems.at[pl.ds(0, 16)], slice(0, units))
    downs = fetches(here_ref, pair, whole, sems.at[pl.ds(16, 16)], slice(units, None))
    fetched(ups)
    fetched(downs)
    step = units // 4
    for at in range(0, units, step):
        lanes = slice(at, at + step)
        value, slope = gelu_parts(dot(n_ref[...], whole[:, lanes]))
        act_ref[:, lanes] = (value * mask_ref[:, lanes]).astype(BF)
        back = dot_t(b_ref[...], whole[at : at + step, units:])
        grad_ref[:, lanes] = (back * (slope * mask_ref[:, lanes])).astype(BF)
    store_parts(dot_t(grad_ref[...], whole[:, :units]), part_refs[4:])
    store_parts(dot(act_ref[...], whole[:, units:]), part_refs[:4])


def block_grads(refs):
    for i in range(len(refs) // 4):
        left, left_near, right, right_near = refs[4 * i : 4 * i + 4]
        total = t_dot(left[...], right[...]) + t_dot(left_near[...], right_near[...])
        yield i, total.reshape(4, total.shape[0] // 4, total.shape[1])


def weight_grad_kernel(here_ref, *refs):
    *refs, out_ref = refs
    done = 0
    for i, total in block_grads(refs[: len(refs) // 4 * 4]):
        rows = total.shape[1]
        out_ref[:, 0, done : done + rows] = total.astype(BF)
        done += rows
    for ref in refs[len(refs) // 4 * 4 :]:
        out_ref[:, 0, done:] = ref[:, 0]


def weight_grads(here, groups, below=()):
    tokens, features = groups[0][0].shape
    columns = groups[0][2].shape[1]
    rows = features // 16 * len(groups) + sum(a.shape[2] for a in below)
    args = [a for group in groups for a in group]
    by_xh = lambda n: pl.BlockSpec((4, 1, n, columns), lambda i, here: (0, i, 0, 0))
    left = pl.BlockSpec((tokens, features // 4), lambda i, here: (0, 2 * i + here[0]))
    right = pl.BlockSpec((tokens, columns), lambda i, here: (0, 0))
    return pl.pallas_call(
        weight_grad_kernel,
        grid_spec=pltpu.PrefetchScalarGridSpec(
            num_scalar_prefetch=1,
            grid=(2,),
            in_specs=[left, left, right, right] * len(groups) + [by_xh(a.shape[2]) for a in below],
            out_specs=by_xh(rows),
        ),
        out_shape=shape((4, 2, rows, columns), BF),
        compiler_params=pltpu.CompilerParams(vmem_limit_bytes=56 * 2**20),
        cost_estimate=LIGHT,
    )(here, *args, *below)


def near(array):
    return shifted(array, "core", 1)


def with_near(arrays):
    return [*arrays, *(near(a) for a in arrays)]


def layer_pairs(shard):
    sec = lax.axis_index("sec")
    places = [(sec, xh) for sec in (0, 1) for xh in (0, 1)]
    across = [(2 * s + x, 2 * (1 - s) + 1 - x) for s, x in places]
    own = jnp.stack([shard, shifted(shard, "xh", 1)])
    other = jnp.stack([shifted(shard, "sec", 1), lax.ppermute(shard, ("sec", "xh"), across)])
    return jnp.where(sec == 0, own, other), jnp.where(sec == 0, other, own)


def y_gathered(pair):
    return lax.all_gather(pair, "y", axis=0, tiled=False)


def scaled(v):
    return (v * norm_scale(v)).astype(BF)


def attention(x, normed, w_out, tables, hook):
    cos, sin, pos_here, pos_whole, unit_mask, here = tables
    x = x.astype(F32)
    w_in, normed = hook(0, normed)
    normed = jnp.concatenate(normed, 0)
    tokens, features = normed.shape
    width = w_in[0].shape[-1] // 3
    queries, kv = call(
        qkv_kernel,
        [shape((tokens, width), BF), shape((tokens, 2 * width), BF)],
        here, normed, cos, sin, rows=features, blocks=w_in,
    )
    kv = hook(1, kv)
    kv = family(kv)
    kv = hook(2, kv)
    mixed, lse, *parts = call(
        attend_kernel,
        [shape((tokens, width), BF), shape((tokens, width), F32), *part_shapes(features)],
        here, queries, kv, pos_here, pos_whole, rows=width, blocks=w_out(),
    )
    parts = hook(3, parts)
    received = hook(7, sent_home(parts))
    middle = x + summed(parts, received)
    return middle, (x, queries, kv, lse, middle), [(a, near(a)) for a in (normed, mixed)], w_in


def feed_gathered(middle, hook):
    return jnp.concatenate(hook(4, gather_ring(scaled(middle), "z")), 0)


def lefts_of(normed, activated):
    return [(a, near(a)) for a in (normed, activated)]


def feed_shapes(features, mask, *types):
    return [shape((256, mask.shape[1]), t) for t in types] + part_shapes(features)


def arrived(middle, parts, received):
    return (middle + summed(parts, received)).astype(BF)


def norm_backward(v, q, straight):
    scale = norm_scale(v)
    n = v * scale
    return straight + scale * (q - n * jnp.mean(q * n, -1, keepdims=True))


def backward(grad_out, branch, kept, feed_back, lefts, weights, tables, hook):
    x, queries, kv, lse, middle = kept
    normed, mixed, normed_two, activated = lefts
    w_in, w_out = weights
    cos, sin, pos_here, pos_whole, unit_mask, here = tables
    tokens, width = queries.shape
    features = x.shape[1]
    grad_out = grad_out.astype(F32)
    grad_up, *parts = feed_back
    received = sent_home(parts)
    feed = weight_grads(
        here,
        [(*normed_two, grad_up, near(grad_up)), (*activated, branch, near(branch))],
    )
    received, feed = tied(received, feed)
    received = hook(1, received, feed)
    grad_middle = norm_backward(middle, summed(parts, received), grad_out)
    ring = gather_ring(grad_middle.astype(BF), "z")
    ring = hook(2, ring)
    branch = jnp.concatenate(ring, 0)
    dq, own, send, far = call(
        attend_back_kernel,
        [
            shape((tokens, width), BF),
            shape((tokens, 2 * width), F32),
            shape((2 * tokens, 2 * width), BF),
            shape((tokens, 2 * width), F32),
        ],
        here, branch, queries, kv, lse, pos_here, pos_whole, cos, sin, rows=width, blocks=w_out,
    )
    dq, own, send, far = hook(6, (dq, own, send, far))
    branch_near = near(branch)
    send = near(send)
    far = (far + send[tokens:].astype(F32)).astype(BF)
    far = shifted(far, "sec", 1)
    out = t_dot(jnp.concatenate(mixed, 0), jnp.concatenate([branch, branch_near], 0)).astype(BF)
    out = lax.dynamic_index_in_dim(out.reshape(2, 2, -1, features), here[0], 1, keepdims=False)
    out = out.reshape(2, 4, -1, features).transpose(1, 0, 2, 3)
    far, out = tied(far, out)
    far = hook(3, far)
    grad_projected, *parts = call(
        project_back_kernel,
        [shape((tokens, 3 * width), BF), *part_shapes(features)],
        here, dq, own, send, far, cos, sin, rows=features, blocks=w_in,
    )
    parts = hook(5, parts)
    received = sent_home(parts)
    out = out.reshape(4, 2, -1, 3 * width)
    g_in = weight_grads(here, [(*normed, grad_projected, near(grad_projected))], [out])
    received, g_in = tied(received, g_in)
    received = hook(4, received, g_in)
    return norm_backward(x, summed(parts, received), grad_middle).astype(BF)


def home_route():
    return [
        ((dp * 4 + y) * 4 + z, (y * 4 + z) * 4 + dp)
        for dp in range(4)
        for y in range(4)
        for z in range(4)
    ]


def local(
    inputs,
    cotangent,
    positions,
    granularity,
    attention_gain,
    attention_in,
    attention_out,
    feed_gain,
    feed_up,
    feed_down,
):
    sec = lax.axis_index("sec")
    rows, width_in = attention_in.shape[1:]
    model = attention_out.shape[2]
    units = feed_up.shape[2]

    core = lax.axis_index("core")

    def layered(mine):
        other = shifted(mine, "sec", 1)
        return jnp.where(sec == 0, mine, other), jnp.where(sec == 0, other, mine)

    def with_gain(weight, gain):
        return (weight.astype(F32) * gain.astype(F32)[:, None]).astype(BF)

    w_in = with_gain(attention_in[0], attention_gain[0])
    w_up = with_gain(feed_up[0], feed_gain[0])
    w_in = w_in.reshape(rows, 3, 4, width_in // 12).transpose(2, 0, 1, 3)
    w_up = w_up.reshape(rows, 16, 4, units // 64).transpose(2, 0, 1, 3)
    both = [w_in.reshape(4, rows, width_in // 4), w_up.reshape(4, rows, units // 4)]
    both = lax.all_to_all(jnp.concatenate(both, 2), "z", 0, 0, tiled=True)
    outs = lax.ppermute(attention_out[0], ("xh", "core", "y", "z"), home_route())
    streams = jnp.stack([inputs, cotangent], 1)
    both, streams, positions, outs = tied(both.reshape(4 * rows, -1), streams, positions, outs)
    attn = jnp.concatenate([both[:, : width_in // 4], outs.reshape(-1, width_in // 4)], 0)
    attn_0, attn_1 = layer_pairs(attn)
    streams = brought(streams)
    feed = jnp.concatenate([both[:, width_in // 4 :], feed_down[0]], 1)
    attn_0, attn_1, (x_0, cotangent) = tied(attn_0, attn_1, streams)
    attn_0 = y_gathered(attn_0)
    feed_0, feed_1 = layer_pairs(feed)
    ring = gather_ring(jnp.stack([scaled(x_0.astype(F32)), cotangent]), "z")
    feed_0, feed_1, ring = tied(feed_0, feed_1, ring)
    normed_0, branch_1 = ([a[i] for a in ring] for i in (0, 1))
    branch_1 = jnp.concatenate(branch_1, 0)
    feed_0 = y_gathered(feed_0)

    def out_rows(attn):
        out = attn[:, :, 4 * rows :].reshape(4, 2, rows, model)
        return with_near([out.transpose(1, 0, 2, 3).reshape(2, 4 * rows, model)])

    y = lax.axis_index("y")
    seq = lambda a: lax.dynamic_index_in_dim(a, y, 0, keepdims=False)
    facts = jnp.concatenate([positions, jnp.broadcast_to(granularity[:, None], (2, 128))], 1)
    other = shifted(facts, "core", 1)
    facts = jnp.where(core == 0, jnp.concatenate([facts, other]), jnp.concatenate([other, facts]))
    facts = seq(facts)
    level = facts[-1]
    pos = rolled(facts[:-128].reshape(2, 2, 4, -1), "z", 2)
    pos = rolled(rolled(pos, "core", 1), "sec", 0).reshape(4, -1)
    here = jnp.stack([core, y, lax.axis_index("xh"), 0])
    half = HEAD // 2
    freqs = jnp.exp(-math.log(THETA) * jnp.arange(half, dtype=F32) / half)
    angles = pos[0].astype(F32)[:, None] * freqs
    cos, sin = jnp.cos(angles), jnp.sin(angles)
    unit_width = (units // 32) * lax.shift_left(1, level)
    tables = (
        jnp.concatenate([cos, cos], 1),
        jnp.concatenate([-sin, sin], 1),
        pos[0][:, None],
        pos.reshape(1, -1),
        (jnp.arange(units // 4) < unit_width).astype(F32)[None],
        here,
    )

    at = {"attn_0": attn_0, "attn_1": attn_1, "feed_0": feed_0, "feed": feed_1}

    def hold(chain, *names):
        values = [at[n] for n in names]
        chain, values = tied(chain, values)
        at.update(zip(names, values))
        return chain

    def forward_0(point, chain, *more):
        if point == 0:
            chain = hold(chain, "attn_0")
            return with_near([at["attn_0"]]), chain
        if point == 1:
            at["out_0"] = out_rows(at["attn_0"])
        if point == 2:
            chain = hold(chain, "attn_1", "feed", "out_0")
            at["attn_1"], at["feed"] = y_gathered(at["attn_1"]), y_gathered(at["feed"])
        if point == 7:
            chain = hold(chain, "feed_0")
            at["feed_0"] = with_near([at["feed_0"]])
        if point == 8:
            chain = hold(chain, "attn_1")
            at["in_1"] = with_near([at["attn_1"]])
        return chain

    def forward_1(point, chain, *more):
        if point == 0:
            chain = hold(chain, "in_1")
            return at["in_1"], chain
        if point == 1:
            at["out_1"] = out_rows(at["attn_1"])
        if point == 2:
            chain = hold(chain, "out_1")
        if point == 3:
            chain = hold(chain, "feed")
            at["feed"] = with_near([at["feed"]])
        return chain

    mask = tables[4]
    middle_0, kept_0, lefts_0, in_0 = attention(
        x_0, normed_0, lambda: at["out_0"], tables, forward_0
    )
    normed = feed_gathered(middle_0, forward_0)
    feed_0 = at["feed_0"]
    activated, slope_0, *parts = call(
        feed_kernel, feed_shapes(model, mask, BF, F32), here, normed, mask, rows=model, blocks=feed_0
    )
    lefts_0 += lefts_of(normed, activated)
    hidden_0 = arrived(middle_0, parts, forward_0(8, sent_home(parts)))
    middle_1, kept_1, lefts_1, in_1 = attention(
        hidden_0, gather_ring(scaled(hidden_0.astype(F32)), "z"), lambda: at["out_1"], tables, forward_1
    )
    normed = feed_gathered(middle_1, forward_1)
    activated, grad_up, *parts = call(
        feed_both_kernel,
        feed_shapes(model, mask, BF, BF) + part_shapes(model),
        here, normed, mask, branch_1, rows=model, blocks=at["feed"],
    )
    lefts_1 += lefts_of(normed, activated)
    parts_1, feed_back_1 = parts[:4], [grad_up, *parts[4:]]
    out_0, out_1 = at["out_0"], at["out_1"]

    def y_sum(grads):
        flat = grads.reshape(-1, grads.shape[-1])
        flat = lax.psum_scatter(flat, "y", scatter_dimension=0, tiled=True)
        return flat.reshape(grads.shape[1:])

    def x_terms(blocks):
        xh = here[2]
        pick = lambda l, x: lax.dynamic_index_in_dim(
            lax.dynamic_index_in_dim(blocks, l, 0, keepdims=False), x, 0, keepdims=False
        )
        places = [(a, x) for a in (0, 1) for x in (0, 1)]
        across = [(2 * a + x, 2 * (1 - a) + 1 - x) for a, x in places]
        return [
            pick(sec, xh),
            shifted(pick(sec, 1 - xh), "xh", 1),
            shifted(pick(1 - sec, xh), "sec", 1),
            lax.ppermute(pick(1 - sec, 1 - xh), ("sec", "xh"), across),
        ]

    def terms(blocks):
        return sum(a.astype(F32) for a in blocks)

    at["parts"] = parts_1

    def backward_1(point, chain, *grads):
        if point == 1:
            at["feed1"] = y_sum(grads[0])
        if point == 2:
            chain = hold(chain, "parts")
            at["received"] = sent_home(at["parts"])
        if point == 3:
            chain = hold(chain, "received")
        if point == 4:
            chain = hold(chain, "feed1")
            at["in1"] = y_sum(grads[0])
        return chain

    def backward_0(point, chain, *grads):
        if point == 1:
            chain = hold(chain, "in1")
            at["feed0"] = y_sum(grads[0])
        if point == 5:
            chain = hold(chain, "feed0")
            feeds = jnp.stack([at["feed0"], at["feed1"]])
            at["up"], at["down"] = (
                x_terms(feeds[:, :, a : a + 4 * rows]) for a in (0, 4 * rows)
            )
        if point == 4:
            at["in0"] = y_sum(grads[0])
        return chain

    grad_1 = backward(
        cotangent, branch_1, kept_1, feed_back_1, lefts_1, (in_1, out_1), tables, backward_1
    )
    hidden_1 = arrived(middle_1, at["parts"], at["received"])
    branch_0 = gathered(grad_1, "z")
    feed_back_0 = call(
        feed_back_kernel, feed_shapes(model, mask, BF), here, branch_0, slope_0, rows=model, blocks=feed_0
    )
    grad_0 = backward(
        grad_1, branch_0, kept_0, feed_back_0, lefts_0, (in_0, out_0), tables, backward_0
    )
    def columns_home(block):
        z = lax.axis_index("z")
        pick = lambda k: lax.dynamic_index_in_dim(block, lax.rem(z + k, 4), 0, keepdims=False)
        got = [pick(0)] + [shifted(pick(k), "z", k) for k in (1, 2, 3)]
        return rolled(jnp.stack(got), "z", 0)

    g_up, g_down = terms(at["up"]), terms(at["down"])
    g_up = columns_home(g_up.astype(BF).reshape(4, rows, -1)).astype(F32)
    g_in, g_out = (
        jnp.stack([at[n][:, rows_of] for n in ("in0", "in1")])
        for rows_of in (slice(0, 4 * rows), slice(4 * rows, None))
    )
    g_in = lax.all_to_all(g_in.reshape(16, rows, -1), ("sec", "xh", "z"), 0, 0, tiled=True)
    g_out = terms(x_terms(g_out.reshape(2, 2, rows, model)))
    g_in, grad_0 = tied(g_in, grad_0)
    g_in = jnp.sum(g_in.reshape(4, 4, rows, -1).astype(F32), 0)
    to_0 = returned(jnp.stack([hidden_0, grad_0]), 0)
    to_1 = returned(jnp.stack([hidden_1, grad_1]), 1)
    hidden, input_grads = (jnp.where(sec == 0, a, b)[None] for a, b in zip(to_0, to_1))
    g_in = g_in.reshape(4, rows, 3, width_in // 12).transpose(1, 2, 0, 3).reshape(rows, width_in)
    g_up = g_up.reshape(4, rows, 16, units // 64).transpose(1, 2, 0, 3).reshape(rows, units)
    back = [(b, a) for a, b in home_route()]
    g_out = lax.ppermute(g_out.astype(BF), ("xh", "core", "y", "z"), back).astype(F32)


    def home(grad, weight, gain):
        return grad * gain.astype(F32)[:, None], jnp.sum(grad * weight.astype(F32), 1)

    g_in, g_gain = home(g_in, attention_in[0], attention_gain[0])
    g_up, g_gain_two = home(g_up, feed_up[0], feed_gain[0])
    return (
        hidden,
        input_grads,
        g_gain[None],
        g_in[None],
        g_out[None],
        g_gain_two[None],
        g_up[None],
        g_down[None],
    )


def solution(mesh):
    fine = Mesh(mesh.devices.reshape(2, 2, 2, 4, 4), EVERY)
    dp, ctx = ("xh", "core"), ("y", "z")
    ranks = dp + ctx
    in_specs = (
        P(dp, ctx, None),
        P(dp, ctx, None),
        P(dp, None),
        P(dp),
        P("sec", ranks),
        P("sec", ranks, None),
        P("sec", ranks, None),
        P("sec", ranks),
        P("sec", ranks, None),
        P("sec", ranks, None),
    )
    out_specs = (
        P("sec", dp, ctx, None),
        P("sec", dp, ctx, None),
        P("sec", ranks),
        P("sec", ranks, None),
        P("sec", ranks, None),
        P("sec", ranks),
        P("sec", ranks, None),
        P("sec", ranks, None),
    )
    return jax.shard_map(local, mesh=fine, in_specs=in_specs, out_specs=out_specs, check_vma=False)
```

```python
import math

import jax
import jax.numpy as jnp
from jax import lax
from jax.experimental import pallas as pl
from jax.experimental.pallas import tpu as pltpu
from jax.sharding import Mesh
from jax.sharding import PartitionSpec as P

HEAD = 128
EPS = 1e-05
THETA = 10000.0
MASKED = -1e30
BF = jnp.bfloat16
F32 = jnp.float32
PLANE = ("xh", "core", "y")
EVERY = ("sec", "xh", "core", "y", "z")


def shifted(block, axis, distance):
    n = lax.axis_size(axis)
    return lax.ppermute(block, axis, [(i, (i + distance) % n) for i in range(n)])


def gather_ring(block, axis):
    return [block] + [shifted(block, axis, k) for k in range(1, lax.axis_size(axis))]


def gathered(block, axis):
    return jnp.concatenate(gather_ring(block, axis), 0)


def scattered(blocks, axis):
    total = blocks[0].astype(F32)
    for k in range(1, lax.axis_size(axis)):
        total = total + shifted(blocks[k].astype(BF), axis, -k).astype(F32)
    return total


def rolled(array, axis_name, dim):
    n = lax.axis_size(axis_name)
    me = lax.axis_index(axis_name)
    return jnp.concatenate(
        [lax.dynamic_slice_in_dim(array, lax.rem(me - k + n, n), 1, dim) for k in range(n)], dim
    )


def family(block):
    near = shifted(block, "core", 1)
    far = shifted(block, "sec", 1)
    return [block, near, far, shifted(far, "core", 1)]


def place(sec, core, y):
    return (sec * 2 + core) * 4 + y


def brought(pair):
    got = []
    for i in (0, 1):
        route = [
            (place(y // 2, core, y), place(y // 2, y % 2, 2 * core + i))
            for core in (0, 1)
            for y in range(4)
        ]
        got.append(lax.ppermute(pair[i], ("sec", "core", "y"), route))
    return jnp.where(lax.axis_index("y") % 2 == 0, got[0], got[1])


def returned(block, layer):
    got = []
    for i in (0, 1):
        route = [
            (place(sec, core, y), place(layer, y // 2, 2 * sec + core))
            for sec in (0, 1)
            for core in (0, 1)
            for y in (i, i + 2)
        ]
        got.append(lax.ppermute(block, ("sec", "core", "y"), route))
    return jnp.stack(got, -3)


def dot(a, b):
    return jnp.dot(a, b, preferred_element_type=F32)


def dot_t(a, b):
    return lax.dot_general(a, b, (((1,), (1,)), ((), ())), preferred_element_type=F32)


def t_dot(a, b):
    return lax.dot_general(a, b, (((0,), (0,)), ((), ())), preferred_element_type=F32)


def norm_scale(v):
    return lax.rsqrt(jnp.mean(v * v, -1, keepdims=True) + EPS)


def gelu_parts(up):
    phi = 0.5 + 0.5 * lax.erf(up * math.sqrt(0.5))
    density = jnp.exp(-0.5 * up * up) * (1.0 / math.sqrt(2.0 * math.pi))
    return up * phi, phi + up * density


def tied(*arrays):
    return lax.optimization_barrier(arrays)


VMEM = pl.BlockSpec(memory_space=pltpu.VMEM)
SMEM = pl.BlockSpec(memory_space=pltpu.SMEM)


LIGHT = pl.CostEstimate(flops=1, bytes_accessed=1, transcendentals=0)


def call(kernel, out_shape, here, *args, rows, blocks, scratch=()):
    return pl.pallas_call(
        kernel,
        out_shape=out_shape,
        in_specs=[SMEM] + [VMEM] * len(args) + [pl.BlockSpec(memory_space=pl.ANY)] * len(blocks),
        out_specs=[VMEM] * len(out_shape),
        scratch_shapes=[*scratch, *fetch_scratch(rows, blocks)],
        compiler_params=pltpu.CompilerParams(vmem_limit_bytes=56 * 2**20),
        cost_estimate=LIGHT,
    )(here, *args, *blocks)


def shape(dims, dtype):
    return jax.ShapeDtypeStruct(dims, dtype)


def part_shapes(features):
    return [shape((64, features), F32)] + [shape((64, features), BF)] * 3


def store_parts(total, refs):
    for k, ref in enumerate(refs):
        ref[...] = total[64 * k : 64 * (k + 1)].astype(ref.dtype)


def summed(parts, received):
    total = parts[0].astype(F32)
    for r in received:
        total = total + r.astype(F32)
    return total


def sent_home(parts):
    return [shifted(parts[k], "z", -k) for k in range(1, 4)]


def stacked(refs, whole):
    rows = refs[0].shape[0]
    for k, ref in enumerate(refs):
        whole[rows * k : rows * (k + 1)] = ref[...]


def swap_halves(v):
    return pltpu.roll(v, HEAD // 2, 1)


def fetches(here_ref, refs, whole, sems, lanes=slice(None)):
    copies = []
    each = len(refs) // 2
    ys = 4 if each > 1 or len(refs[0].shape) == 4 else 1
    for i, ref in enumerate(refs):
        core = here_ref[0] if i < each else 1 - here_ref[0]
        for j in range(ys // each):
            part = ref.at[j] if len(ref.shape) == 4 else ref
            y = j if each == 1 else lax.rem(here_ref[1] + 4 - i % each, 4)
            block = whole.shape[0] // (4 * ys)
            for dx in (0, 1):
                xh = lax.rem(here_ref[2] + dx, 2)
                at = pl.multiple_of(((2 * xh + core) * ys + y) * block, 32)
                copy = pltpu.make_async_copy(
                    part.at[dx, pl.ds(0, block), lanes],
                    whole.at[pl.ds(at, block), lanes],
                    sems.at[len(copies)],
                )
                copy.start()
                copies.append(copy)
    return copies


def fetched(copies):
    for copy in copies:
        copy.wait()


def fetch_scratch(rows, blocks):
    return [pltpu.VMEM((rows, blocks[0].shape[-1]), BF), pltpu.SemaphoreType.DMA((32,))]


def qkv_kernel(here_ref, n0, n1, n2, n3, cos_ref, sin_ref, *refs):
    *refs, n_ref, q_ref, kv_ref, whole, sems = refs
    copies = fetches(here_ref, refs, whole, sems)
    stacked((n0, n1, n2, n3), n_ref)
    fetched(copies)
    width = q_ref.shape[1]
    cos, sin = cos_ref[...], sin_ref[...]
    for j in (0, 1, 2):
        ref, at = (q_ref, 0) if j == 0 else (kv_ref, (j - 1) * width)
        total = dot(n_ref[...], whole[:, j * width : (j + 1) * width])
        for h in range(0, width, HEAD):
            v = total[:, h : h + HEAD]
            if j < 2:
                v = v * cos + swap_halves(v) * sin
            ref[:, at + h : at + h + HEAD] = v.astype(BF)


def masked_scores(q, k, visible):
    return jnp.where(visible, dot_t(q, k) * (1.0 / math.sqrt(HEAD)), MASKED)


def attend_kernel(
    here_ref, q_ref, kv0, kv1, kv2, kv3, pq_ref, pk_ref, mine_ref, other_ref, mixed_ref, lse_ref,
    *refs,
):
    *part_refs, kv_ref, whole, sems = refs
    copies = fetches(here_ref, (mine_ref, other_ref), whole, sems)
    stacked((kv0, kv1, kv2, kv3), kv_ref)
    width = q_ref.shape[1]
    visible = pk_ref[...] <= pq_ref[...]
    for i in range(width // HEAD):
        h = slice(i * HEAD, (i + 1) * HEAD)
        scores = masked_scores(q_ref[:, h], kv_ref[:, h], visible)
        most = jnp.max(scores, -1, keepdims=True)
        exponent = jnp.exp(scores - most)
        total = jnp.sum(exponent, -1, keepdims=True)
        probs = (exponent / total).astype(BF)
        values = kv_ref[:, width + i * HEAD : width + (i + 1) * HEAD]
        mixed_ref[:, h] = dot(probs, values).astype(BF)
        lse_ref[:, h] = jnp.broadcast_to(most + jnp.log(total), (q_ref.shape[0], HEAD))
    fetched(copies)
    store_parts(dot(mixed_ref[...], whole[...]), part_refs)


def attend_back_kernel(
    here_ref, b0, b1, b2, b3, q_ref, kv0, kv1, kv2, kv3, lse_ref, pq_ref, pk_ref, cos_ref, sin_ref,
    mine_ref, other_ref, b_ref, dq_ref, own_ref, send_ref, far_ref, kv_ref, whole, sems,
):
    copies = fetches(here_ref, (mine_ref, other_ref), whole, sems)
    stacked((b0, b1, b2, b3), b_ref)
    stacked((kv0, kv1, kv2, kv3), kv_ref)
    fetched(copies)
    tokens, width = q_ref.shape
    scale = 1.0 / math.sqrt(HEAD)
    visible = pk_ref[...] <= pq_ref[...]
    grad_mixed = dot_t(b_ref[...], whole[...]).astype(BF)
    for i in range(width // HEAD):
        h = slice(i * HEAD, (i + 1) * HEAD)
        vh = slice(width + i * HEAD, width + (i + 1) * HEAD)
        q, k, v, g = q_ref[:, h], kv_ref[:, h], kv_ref[:, vh], grad_mixed[:, h]
        probs = jnp.exp(masked_scores(q, k, visible) - lse_ref[:, i * HEAD : i * HEAD + 1])
        grad_probs = dot_t(g, v)
        weighted = jnp.sum(probs * grad_probs, -1, keepdims=True)
        grad_scores = (probs * (grad_probs - weighted)).astype(BF)
        dq = dot(grad_scores, k) * scale
        dq_ref[:, h] = (dq * cos_ref[...] - swap_halves(dq) * sin_ref[...]).astype(BF)
        for lanes, grad in (
            (h, t_dot(grad_scores, q) * scale),
            (vh, t_dot(probs.astype(BF), g)),
        ):
            own_ref[:, lanes] = grad[:tokens]
            send_ref[:tokens, lanes] = grad[tokens : 2 * tokens].astype(BF)
            far_ref[:, lanes] = grad[2 * tokens : 3 * tokens].astype(BF)
            send_ref[tokens:, lanes] = grad[3 * tokens :].astype(BF)


def project_back_kernel(here_ref, dq_ref, own_ref, near_ref, far_ref, cos_ref, sin_ref, *refs):
    *refs, grad_ref, p0, p1, p2, p3, whole, sems = refs
    part_refs = (p0, p1, p2, p3)
    copies = fetches(here_ref, refs, whole, sems)
    width = dq_ref.shape[1]
    grad_ref[:, :width] = dq_ref[...]
    for h in range(0, 2 * width, HEAD):
        lanes = slice(h, h + HEAD)
        near = near_ref[: dq_ref.shape[0], lanes]
        v = own_ref[:, lanes] + near.astype(F32) + far_ref[:, lanes].astype(F32)
        if h < width:
            v = v * cos_ref[...] - swap_halves(v) * sin_ref[...]
        grad_ref[:, width + h : width + h + HEAD] = v.astype(BF)
    fetched(copies)
    store_parts(dot_t(grad_ref[...], whole[...]), part_refs)


def feed_kernel(
    here_ref, n0, n1, n2, n3, mask_ref, mine_ref, other_ref, n_ref, act_ref, slope_ref, *refs
):
    *part_refs, whole, sems = refs
    units = act_ref.shape[1]
    pair = (mine_ref, other_ref)
    ups = fetches(here_ref, pair, whole, sems.at[pl.ds(0, 16)], slice(0, units))
    downs = fetches(here_ref, pair, whole, sems.at[pl.ds(16, 16)], slice(units, None))
    stacked((n0, n1, n2, n3), n_ref)
    fetched(ups)
    step = units // 4
    for at in range(0, units, step):
        lanes = slice(at, at + step)
        value, slope = gelu_parts(dot(n_ref[...], whole[:, lanes]))
        act_ref[:, lanes] = (value * mask_ref[:, lanes]).astype(BF)
        slope_ref[:, lanes] = slope * mask_ref[:, lanes]
    fetched(downs)
    store_parts(dot(act_ref[...], whole[:, units:]), part_refs)


def feed_back_kernel(
    here_ref, b0, b1, b2, b3, slope_ref, mine_ref, other_ref, b_ref, grad_ref, *refs
):
    *part_refs, whole, sems = refs
    units = grad_ref.shape[1]
    pair = (mine_ref, other_ref)
    downs = fetches(here_ref, pair, whole, sems.at[pl.ds(16, 16)], slice(units, None))
    ups = fetches(here_ref, pair, whole, sems.at[pl.ds(0, 16)], slice(0, units))
    stacked((b0, b1, b2, b3), b_ref)
    fetched(downs)
    grad_ref[...] = (dot_t(b_ref[...], whole[:, units:]) * slope_ref[...]).astype(BF)
    fetched(ups)
    store_parts(dot_t(grad_ref[...], whole[:, :units]), part_refs)


def feed_both_kernel(
    here_ref, n0, n1, n2, n3, mask_ref, b_ref, mine_ref, other_ref, n_ref, act_ref, grad_ref, *refs
):
    *part_refs, whole, sems = refs
    units = act_ref.shape[1]
    pair = (mine_ref, other_ref)
    ups = fetches(here_ref, pair, whole, sems.at[pl.ds(0, 16)], slice(0, units))
    downs = fetches(here_ref, pair, whole, sems.at[pl.ds(16, 16)], slice(units, None))
    stacked((n0, n1, n2, n3), n_ref)
    fetched(ups)
    fetched(downs)
    step = units // 4
    for at in range(0, units, step):
        lanes = slice(at, at + step)
        value, slope = gelu_parts(dot(n_ref[...], whole[:, lanes]))
        act_ref[:, lanes] = (value * mask_ref[:, lanes]).astype(BF)
        back = dot_t(b_ref[...], whole[at : at + step, units:])
        grad_ref[:, lanes] = (back * (slope * mask_ref[:, lanes])).astype(BF)
    store_parts(dot_t(grad_ref[...], whole[:, :units]), part_refs[4:])
    store_parts(dot(act_ref[...], whole[:, units:]), part_refs[:4])


def block_grads(refs):
    for i in range(len(refs) // 4):
        left, left_near, right, right_near = refs[4 * i : 4 * i + 4]
        total = t_dot(left[...], right[...]) + t_dot(left_near[...], right_near[...])
        yield i, total.reshape(4, total.shape[0] // 4, total.shape[1])


def weight_grad_kernel(here_ref, *refs):
    *refs, out_ref = refs
    done = 0
    for i, total in block_grads(refs[: len(refs) // 4 * 4]):
        rows = total.shape[1]
        out_ref[:, 0, done : done + rows] = total.astype(BF)
        done += rows
    for ref in refs[len(refs) // 4 * 4 :]:
        out_ref[:, 0, done:] = ref[:, 0]


def weight_grads(here, groups, below=()):
    tokens, features = groups[0][0].shape
    columns = groups[0][2].shape[1]
    rows = features // 16 * len(groups) + sum(a.shape[2] for a in below)
    args = [a for group in groups for a in group]
    by_xh = lambda n: pl.BlockSpec((4, 1, n, columns), lambda i, here: (0, i, 0, 0))
    left = pl.BlockSpec((tokens, features // 4), lambda i, here: (0, 2 * i + here[0]))
    right = pl.BlockSpec((tokens, columns), lambda i, here: (0, 0))
    return pl.pallas_call(
        weight_grad_kernel,
        grid_spec=pltpu.PrefetchScalarGridSpec(
            num_scalar_prefetch=1,
            grid=(2,),
            in_specs=[left, left, right, right] * len(groups) + [by_xh(a.shape[2]) for a in below],
            out_specs=by_xh(rows),
        ),
        out_shape=shape((4, 2, rows, columns), BF),
        compiler_params=pltpu.CompilerParams(vmem_limit_bytes=56 * 2**20),
        cost_estimate=LIGHT,
    )(here, *args, *below)


def near(array):
    return shifted(array, "core", 1)


def with_near(arrays):
    return [*arrays, *(near(a) for a in arrays)]


def layer_pairs(shard):
    sec = lax.axis_index("sec")
    places = [(sec, xh) for sec in (0, 1) for xh in (0, 1)]
    across = [(2 * s + x, 2 * (1 - s) + 1 - x) for s, x in places]
    own = jnp.stack([shard, shifted(shard, "xh", 1)])
    other = jnp.stack([shifted(shard, "sec", 1), lax.ppermute(shard, ("sec", "xh"), across)])
    return jnp.where(sec == 0, own, other), jnp.where(sec == 0, other, own)


def y_gathered(pair):
    return lax.all_gather(pair, "y", axis=0, tiled=False)


def scaled(v):
    return (v * norm_scale(v)).astype(BF)


def attention(x, normed, w_out, tables, hook):
    cos, sin, pos_here, pos_whole, unit_mask, here = tables
    x = x.astype(F32)
    w_in, normed = hook(0, normed)
    tokens, features = 4 * x.shape[0], x.shape[1]
    width = w_in[0].shape[-1] // 3
    normed, queries, kv = call(
        qkv_kernel,
        [shape((tokens, features), BF), shape((tokens, width), BF), shape((tokens, 2 * width), BF)],
        here, *normed, cos, sin, rows=features, blocks=w_in,
    )
    kv = hook(1, kv)
    kv = family(kv)
    kv = hook(2, kv)
    mixed, lse, *parts = call(
        attend_kernel,
        [shape((tokens, width), BF), shape((tokens, width), F32), *part_shapes(features)],
        here, queries, *kv, pos_here, pos_whole, rows=width, blocks=w_out(),
        scratch=[pltpu.VMEM((4 * tokens, 2 * width), BF)],
    )
    parts = hook(3, parts)
    received = hook(7, sent_home(parts))
    middle = x + summed(parts, received)
    return middle, (x, queries, kv, lse, middle), [(a, near(a)) for a in (normed, mixed)], w_in


def lefts_of(normed, activated):
    return [(a, near(a)) for a in (normed, activated)]


def feed_shapes(features, mask, *types):
    by_unit = [shape((256, mask.shape[1]), t) for t in types]
    return [shape((256, features), BF), *by_unit, *part_shapes(features)]


def arrived(middle, parts, received):
    return (middle + summed(parts, received)).astype(BF)


def norm_backward(v, q, straight):
    scale = norm_scale(v)
    n = v * scale
    return straight + scale * (q - n * jnp.mean(q * n, -1, keepdims=True))


def backward(grad_out, branch, kept, feed_back, lefts, weights, tables, hook, last):
    x, queries, kv, lse, middle = kept
    normed, mixed, normed_two, activated = lefts
    w_in, w_out = weights
    cos, sin, pos_here, pos_whole, unit_mask, here = tables
    tokens, width = queries.shape
    features = x.shape[1]
    grad_out = grad_out.astype(F32)
    grad_up, *parts = feed_back
    received = sent_home(parts)
    feed = weight_grads(
        here,
        [(*normed_two, grad_up, near(grad_up)), (*activated, branch, near(branch))],
    )
    received, feed = tied(received, feed)
    received = hook(1, received, feed)
    grad_middle = norm_backward(middle, summed(parts, received), grad_out)
    ring = gather_ring(grad_middle.astype(BF), "z")
    ring = hook(2, ring)
    branch, dq, own, send, far = call(
        attend_back_kernel,
        [
            shape((tokens, features), BF),
            shape((tokens, width), BF),
            shape((tokens, 2 * width), F32),
            shape((2 * tokens, 2 * width), BF),
            shape((tokens, 2 * width), BF),
        ],
        here, *ring, queries, *kv, lse, pos_here, pos_whole, cos, sin, rows=width, blocks=w_out,
        scratch=[pltpu.VMEM((4 * tokens, 2 * width), BF)],
    )
    dq, own, send, far = hook(6, (dq, own, send, far))
    branch_near = near(branch)
    send = near(send)
    far = (far.astype(F32) + send[tokens:].astype(F32)).astype(BF)
    far = shifted(far, "sec", 1)
    out = t_dot(jnp.concatenate(mixed, 0), jnp.concatenate([branch, branch_near], 0)).astype(BF)
    out = lax.dynamic_index_in_dim(out.reshape(2, 2, -1, features), here[0], 1, keepdims=False)
    out = out.reshape(2, 4, -1, features).transpose(1, 0, 2, 3)
    out = out.reshape(4, 2, -1, 3 * width)
    far, out = tied(far, out)
    far = hook(3, far)
    grad_projected, *parts = call(
        project_back_kernel,
        [shape((tokens, 3 * width), BF), *part_shapes(features)],
        here, dq, own, send, far, cos, sin, rows=features, blocks=w_in,
    )
    parts, grad_projected = hook(5, (parts, grad_projected))
    g_in = weight_grads(here, [(*normed, grad_projected, near(grad_projected))], [out])
    if last:
        hook(4, None, g_in)
        received = sent_home(parts)
    else:
        received, g_in = tied(sent_home(parts), g_in)
        received = hook(4, received, g_in)
    return norm_backward(x, summed(parts, received), grad_middle).astype(BF)


def home_route():
    return [
        ((dp * 4 + y) * 4 + z, (y * 4 + z) * 4 + dp)
        for dp in range(4)
        for y in range(4)
        for z in range(4)
    ]


def local(
    inputs,
    cotangent,
    positions,
    granularity,
    attention_gain,
    attention_in,
    attention_out,
    feed_gain,
    feed_up,
    feed_down,
):
    sec = lax.axis_index("sec")
    rows, width_in = attention_in.shape[1:]
    model = attention_out.shape[2]
    units = feed_up.shape[2]

    core = lax.axis_index("core")

    def layered(mine):
        other = shifted(mine, "sec", 1)
        return jnp.where(sec == 0, mine, other), jnp.where(sec == 0, other, mine)

    def with_gain(weight, gain):
        return (weight.astype(F32) * gain.astype(F32)[:, None]).astype(BF)

    w_in = with_gain(attention_in[0], attention_gain[0])
    w_up = with_gain(feed_up[0], feed_gain[0])
    w_in = w_in.reshape(rows, 3, 4, width_in // 12).transpose(2, 0, 1, 3)
    w_up = w_up.reshape(rows, 16, 4, units // 64).transpose(2, 0, 1, 3)
    both = [w_in.reshape(4, rows, width_in // 4), w_up.reshape(4, rows, units // 4)]
    both = lax.all_to_all(jnp.concatenate(both, 2), "z", 0, 0, tiled=True)
    outs = lax.ppermute(attention_out[0], ("xh", "core", "y", "z"), home_route())
    streams = jnp.stack([inputs, cotangent], 1)
    both, streams, positions, outs = tied(both.reshape(4 * rows, -1), streams, positions, outs)
    attn = jnp.concatenate([both[:, : width_in // 4], outs.reshape(-1, width_in // 4)], 0)
    attn_0, attn_1 = layer_pairs(attn)
    streams = brought(streams)
    feed = jnp.concatenate([both[:, width_in // 4 :], feed_down[0]], 1)
    attn_0, attn_1, (x_0, cotangent) = tied(attn_0, attn_1, streams)
    attn_0 = y_gathered(attn_0)
    feed_0, feed_1 = layer_pairs(feed)
    ring = gather_ring(jnp.stack([scaled(x_0.astype(F32)), cotangent]), "z")
    feed_0, feed_1, ring = tied(feed_0, feed_1, ring)
    normed_0, branch_1 = ([a[i] for a in ring] for i in (0, 1))
    branch_1 = jnp.concatenate(branch_1, 0)
    feed_0 = y_gathered(feed_0)

    def out_rows(attn):
        out = attn[:, :, 4 * rows :].reshape(4, 2, rows, model)
        return with_near([out.transpose(1, 0, 2, 3).reshape(2, 4 * rows, model)])

    y = lax.axis_index("y")
    seq = lambda a: lax.dynamic_index_in_dim(a, y, 0, keepdims=False)
    facts = jnp.concatenate([positions, jnp.broadcast_to(granularity[:, None], (2, 128))], 1)
    other = shifted(facts, "core", 1)
    facts = jnp.where(core == 0, jnp.concatenate([facts, other]), jnp.concatenate([other, facts]))
    facts = seq(facts)
    level = facts[-1]
    pos = rolled(facts[:-128].reshape(2, 2, 4, -1), "z", 2)
    pos = rolled(rolled(pos, "core", 1), "sec", 0).reshape(4, -1)
    here = jnp.stack([core, y, lax.axis_index("xh"), 0])
    half = HEAD // 2
    freqs = jnp.exp(-math.log(THETA) * jnp.arange(half, dtype=F32) / half)
    angles = pos[0].astype(F32)[:, None] * freqs
    cos, sin = jnp.cos(angles), jnp.sin(angles)
    unit_width = (units // 32) * lax.shift_left(1, level)
    tables = (
        jnp.concatenate([cos, cos], 1),
        jnp.concatenate([-sin, sin], 1),
        pos[0][:, None],
        pos.reshape(1, -1),
        (jnp.arange(units // 4) < unit_width).astype(F32)[None],
        here,
    )

    at = {"attn_0": attn_0, "attn_1": attn_1, "feed_0": feed_0, "feed": feed_1}

    def hold(chain, *names):
        values = [at[n] for n in names]
        chain, values = tied(chain, values)
        at.update(zip(names, values))
        return chain

    def forward_0(point, chain, *more):
        if point == 0:
            chain = hold(chain, "attn_0")
            return with_near([at["attn_0"]]), chain
        if point == 1:
            at["out_0"] = out_rows(at["attn_0"])
        if point == 2:
            chain = hold(chain, "attn_1", "feed", "out_0")
            at["attn_1"], at["feed"] = y_gathered(at["attn_1"]), y_gathered(at["feed"])
        if point == 7:
            chain = hold(chain, "feed_0")
            at["feed_0"] = with_near([at["feed_0"]])
        if point == 8:
            chain = hold(chain, "attn_1")
            at["in_1"] = with_near([at["attn_1"]])
        return chain

    def forward_1(point, chain, *more):
        if point == 0:
            chain = hold(chain, "in_1")
            return at["in_1"], chain
        if point == 1:
            at["out_1"] = out_rows(at["attn_1"])
        if point == 2:
            chain = hold(chain, "out_1")
        if point == 7:
            chain = hold(chain, "feed")
            at["feed"] = with_near([at["feed"]])
        return chain

    mask = tables[4]
    middle_0, kept_0, lefts_0, in_0 = attention(
        x_0, normed_0, lambda: at["out_0"], tables, forward_0
    )
    normed = forward_0(4, gather_ring(scaled(middle_0), "z"))
    feed_0 = at["feed_0"]
    normed, activated, slope_0, *parts = call(
        feed_kernel, feed_shapes(model, mask, BF, F32), here, *normed, mask, rows=model, blocks=feed_0
    )
    lefts_0 += lefts_of(normed, activated)
    hidden_0 = forward_0(8, arrived(middle_0, parts, sent_home(parts)))
    middle_1, kept_1, lefts_1, in_1 = attention(
        hidden_0, gather_ring(scaled(hidden_0.astype(F32)), "z"), lambda: at["out_1"], tables, forward_1
    )
    normed = forward_1(4, gather_ring(scaled(middle_1), "z"))
    normed, activated, grad_up, *parts = call(
        feed_both_kernel,
        feed_shapes(model, mask, BF, BF) + part_shapes(model),
        here, *normed, mask, branch_1, rows=model, blocks=at["feed"],
    )
    lefts_1 += lefts_of(normed, activated)
    parts_1, feed_back_1 = parts[:4], [grad_up, *parts[4:]]
    out_0, out_1 = at["out_0"], at["out_1"]

    def y_sum(grads):
        flat = grads.reshape(-1, grads.shape[-1])
        flat = lax.psum_scatter(flat, "y", scatter_dimension=0, tiled=True)
        return flat.reshape(grads.shape[1:])

    def x_terms(blocks):
        xh = here[2]
        pick = lambda l, x: lax.dynamic_index_in_dim(
            lax.dynamic_index_in_dim(blocks, l, 0, keepdims=False), x, 0, keepdims=False
        )
        places = [(a, x) for a in (0, 1) for x in (0, 1)]
        across = [(2 * a + x, 2 * (1 - a) + 1 - x) for a, x in places]
        return [
            pick(sec, xh),
            shifted(pick(sec, 1 - xh), "xh", 1),
            shifted(pick(1 - sec, xh), "sec", 1),
            lax.ppermute(pick(1 - sec, 1 - xh), ("sec", "xh"), across),
        ]

    def terms(blocks):
        return sum(a.astype(F32) for a in blocks)

    at["parts"] = parts_1

    def backward_1(point, chain, *grads):
        if point == 1:
            at["feed1"] = y_sum(grads[0])
        if point == 2:
            chain = hold(chain, "parts")
            at["received"] = sent_home(at["parts"])
        if point == 3:
            chain = hold(chain, "received")
        if point == 4:
            chain = hold(chain, "feed1")
            at["in1"] = y_sum(grads[0])
        return chain

    def backward_0(point, chain, *grads):
        if point == 1:
            chain = hold(chain, "in1")
            at["feed0"] = y_sum(grads[0])
        if point == 5:
            chain = hold(chain, "feed0")
            feeds = jnp.stack([at["feed0"], at["feed1"]])
            at["up"], down = tied(x_terms(feeds[:, :, : 4 * rows]), feeds[:, :, 4 * rows :])
            at["down"] = x_terms(down)
        if point == 4:
            g_in, at["to_1"] = tied(grads[0], at["to_1"])
            at["in0"] = y_sum(g_in)
        return chain

    grad_1 = backward(
        cotangent, branch_1, kept_1, feed_back_1, lefts_1, (in_1, out_1), tables, backward_1, False
    )
    hidden_1 = arrived(middle_1, at["parts"], at["received"])
    at["to_1"] = jnp.stack([hidden_1, grad_1])
    branch_0, *feed_back_0 = call(
        feed_back_kernel,
        feed_shapes(model, mask, BF),
        here, *gather_ring(grad_1, "z"), slope_0, rows=model, blocks=feed_0,
    )
    grad_0 = backward(
        grad_1, branch_0, kept_0, feed_back_0, lefts_0, (in_0, out_0), tables, backward_0, True
    )
    def columns_home(block):
        z = lax.axis_index("z")
        pick = lambda k: lax.dynamic_index_in_dim(block, lax.rem(z + k, 4), 0, keepdims=False)
        got = [pick(0)] + [shifted(pick(k), "z", k) for k in (1, 2, 3)]
        return rolled(jnp.stack(got), "z", 0)

    g_up = columns_home(terms(at["up"]).astype(BF).reshape(4, rows, -1))
    g_in, g_out = (
        jnp.stack([at[n][:, rows_of] for n in ("in0", "in1")])
        for rows_of in (slice(0, 4 * rows), slice(4 * rows, None))
    )
    g_in = lax.all_to_all(g_in.reshape(16, rows, -1), ("sec", "xh", "z"), 0, 0, tiled=True)
    g_out = terms(x_terms(g_out.reshape(2, 2, rows, model)))
    g_in, grad_0, g_up, at["down"] = tied(g_in, grad_0, g_up, at["down"])
    g_up, g_down = g_up.astype(F32), terms(at["down"])
    g_in = jnp.sum(g_in.reshape(4, 4, rows, -1).astype(F32), 0)
    to_0 = returned(jnp.stack([hidden_0, grad_0]), 0)
    to_1 = returned(at["to_1"], 1)
    hidden, input_grads = (jnp.where(sec == 0, a, b)[None] for a, b in zip(to_0, to_1))
    g_in = g_in.reshape(4, rows, 3, width_in // 12).transpose(1, 2, 0, 3).reshape(rows, width_in)
    g_up = g_up.reshape(4, rows, 16, units // 64).transpose(1, 2, 0, 3).reshape(rows, units)
    back = [(b, a) for a, b in home_route()]
    g_out = lax.ppermute(g_out.astype(BF), ("xh", "core", "y", "z"), back).astype(F32)


    def home(grad, weight, gain):
        return grad * gain.astype(F32)[:, None], jnp.sum(grad * weight.astype(F32), 1)

    g_in, g_gain = home(g_in, attention_in[0], attention_gain[0])
    g_up, g_gain_two = home(g_up, feed_up[0], feed_gain[0])
    return (
        hidden,
        input_grads,
        g_gain[None],
        g_in[None],
        g_out[None],
        g_gain_two[None],
        g_up[None],
        g_down[None],
    )


def solution(mesh):
    fine = Mesh(mesh.devices.reshape(2, 2, 2, 4, 4), EVERY)
    dp, ctx = ("xh", "core"), ("y", "z")
    ranks = dp + ctx
    in_specs = (
        P(dp, ctx, None),
        P(dp, ctx, None),
        P(dp, None),
        P(dp),
        P("sec", ranks),
        P("sec", ranks, None),
        P("sec", ranks, None),
        P("sec", ranks),
        P("sec", ranks, None),
        P("sec", ranks, None),
    )
    out_specs = (
        P("sec", dp, ctx, None),
        P("sec", dp, ctx, None),
        P("sec", ranks),
        P("sec", ranks, None),
        P("sec", ranks, None),
        P("sec", ranks),
        P("sec", ranks, None),
        P("sec", ranks, None),
    )
    return jax.shard_map(local, mesh=fine, in_specs=in_specs, out_specs=out_specs, check_vma=False)
```

```python
import math

import jax
import jax.numpy as jnp
from jax import lax
from jax.experimental import pallas as pl
from jax.experimental.pallas import tpu as pltpu
from jax.sharding import Mesh
from jax.sharding import PartitionSpec as P

HEAD = 128
EPS = 1e-05
THETA = 10000.0
MASKED = -1e30
BF = jnp.bfloat16
F32 = jnp.float32
PLANE = ("xh", "core", "y")
EVERY = ("sec", "xh", "core", "y", "z")


def shifted(block, axis, distance):
    n = lax.axis_size(axis)
    return lax.ppermute(block, axis, [(i, (i + distance) % n) for i in range(n)])


def gather_ring(block, axis):
    farthest_first = {k: shifted(block, axis, k) for k in (2, 1, 3)}
    return [block] + [farthest_first[k] for k in (1, 2, 3)]


def gathered(block, axis):
    return jnp.concatenate(gather_ring(block, axis), 0)


def scattered(blocks, axis):
    total = blocks[0].astype(F32)
    for k in range(1, lax.axis_size(axis)):
        total = total + shifted(blocks[k].astype(BF), axis, -k).astype(F32)
    return total


def rolled(array, axis_name, dim):
    n = lax.axis_size(axis_name)
    me = lax.axis_index(axis_name)
    return jnp.concatenate(
        [lax.dynamic_slice_in_dim(array, lax.rem(me - k + n, n), 1, dim) for k in range(n)], dim
    )


def family(block):
    near = shifted(block, "core", 1)
    far = shifted(block, "sec", 1)
    return [block, near, far, shifted(far, "core", 1)]


def place(sec, core, y):
    return (sec * 2 + core) * 4 + y


def brought(pair):
    got = []
    for i in (0, 1):
        route = [
            (place(y // 2, core, y), place(y // 2, y % 2, 2 * core + i))
            for core in (0, 1)
            for y in range(4)
        ]
        got.append(lax.ppermute(pair[i], ("sec", "core", "y"), route))
    return jnp.where(lax.axis_index("y") % 2 == 0, got[0], got[1])


def returned(block, layer):
    got = []
    for i in (0, 1):
        route = [
            (place(sec, core, y), place(layer, y // 2, 2 * sec + core))
            for sec in (0, 1)
            for core in (0, 1)
            for y in (i, i + 2)
        ]
        got.append(lax.ppermute(block, ("sec", "core", "y"), route))
    return jnp.stack(got, -3)


def dot(a, b):
    return jnp.dot(a, b, preferred_element_type=F32)


def dot_t(a, b):
    return lax.dot_general(a, b, (((1,), (1,)), ((), ())), preferred_element_type=F32)


def t_dot(a, b):
    return lax.dot_general(a, b, (((0,), (0,)), ((), ())), preferred_element_type=F32)


def norm_scale(v):
    return lax.rsqrt(jnp.mean(v * v, -1, keepdims=True) + EPS)


def gelu_parts(up):
    phi = 0.5 + 0.5 * lax.erf(up * math.sqrt(0.5))
    density = jnp.exp(-0.5 * up * up) * (1.0 / math.sqrt(2.0 * math.pi))
    return up * phi, phi + up * density


def tied(*arrays):
    return lax.optimization_barrier(arrays)


VMEM = pl.BlockSpec(memory_space=pltpu.VMEM)
SMEM = pl.BlockSpec(memory_space=pltpu.SMEM)


LIGHT = pl.CostEstimate(flops=1, bytes_accessed=1, transcendentals=0)


def call(kernel, out_shape, here, *args, rows, blocks, scratch=()):
    return pl.pallas_call(
        kernel,
        out_shape=out_shape,
        in_specs=[SMEM] + [VMEM] * len(args) + [pl.BlockSpec(memory_space=pl.ANY)] * len(blocks),
        out_specs=[VMEM] * len(out_shape),
        scratch_shapes=[*scratch, *fetch_scratch(rows, blocks)],
        compiler_params=pltpu.CompilerParams(vmem_limit_bytes=56 * 2**20),
        cost_estimate=LIGHT,
    )(here, *args, *blocks)


def shape(dims, dtype):
    return jax.ShapeDtypeStruct(dims, dtype)


def part_shapes(features):
    return [shape((64, features), F32)] + [shape((64, features), BF)] * 3


def store_parts(total, refs):
    for k, ref in enumerate(refs):
        ref[...] = total[64 * k : 64 * (k + 1)].astype(ref.dtype)


def summed(parts, received):
    total = parts[0].astype(F32)
    for r in received:
        total = total + r.astype(F32)
    return total


def sent_home(parts):
    return [shifted(parts[k], "z", -k) for k in (2, 1, 3)]


def stacked(refs, whole):
    rows = refs[0].shape[0]
    for k, ref in enumerate(refs):
        whole[rows * k : rows * (k + 1)] = ref[...]


def swap_halves(v):
    return pltpu.roll(v, HEAD // 2, 1)


def fetches(here_ref, refs, whole, sems, lanes=slice(None)):
    copies = []
    each = len(refs) // 2
    ys = 4 if each > 1 or len(refs[0].shape) == 4 else 1
    for i, ref in enumerate(refs):
        core = here_ref[0] if i < each else 1 - here_ref[0]
        for j in range(ys // each):
            part = ref.at[j] if len(ref.shape) == 4 else ref
            y = j if each == 1 else lax.rem(here_ref[1] + 4 - i % each, 4)
            block = whole.shape[0] // (4 * ys)
            for dx in (0, 1):
                xh = lax.rem(here_ref[2] + dx, 2)
                at = pl.multiple_of(((2 * xh + core) * ys + y) * block, 32)
                copy = pltpu.make_async_copy(
                    part.at[dx, pl.ds(0, block), lanes],
                    whole.at[pl.ds(at, block), lanes],
                    sems.at[len(copies)],
                )
                copy.start()
                copies.append(copy)
    return copies


def fetched(copies):
    for copy in copies:
        copy.wait()


def fetch_scratch(rows, blocks):
    return [pltpu.VMEM((rows, blocks[0].shape[-1]), BF), pltpu.SemaphoreType.DMA((48,))]


def qkv_kernel(here_ref, n0, n1, n2, n3, cos_ref, sin_ref, *refs):
    *refs, n_ref, q_ref, kv_ref, whole, sems = refs
    width = q_ref.shape[1]
    copies = [
        fetches(here_ref, refs, whole, sems.at[pl.ds(16 * j, 16)], slice(j * width, (j + 1) * width))
        for j in (0, 1, 2)
    ]
    stacked((n0, n1, n2, n3), n_ref)
    cos, sin = cos_ref[...], sin_ref[...]
    for j in (0, 1, 2):
        fetched(copies[j])
        ref, at = (q_ref, 0) if j == 0 else (kv_ref, (j - 1) * width)
        total = dot(n_ref[...], whole[:, j * width : (j + 1) * width])
        for h in range(0, width, HEAD):
            v = total[:, h : h + HEAD]
            if j < 2:
                v = v * cos + swap_halves(v) * sin
            ref[:, at + h : at + h + HEAD] = v.astype(BF)


def masked_scores(q, k, visible):
    return jnp.where(visible, dot_t(q, k) * (1.0 / math.sqrt(HEAD)), MASKED)


def attend_kernel(
    here_ref, q_ref, kv0, kv1, kv2, kv3, pq_ref, pk_ref, mine_ref, other_ref, mixed_ref, lse_ref,
    *refs,
):
    *part_refs, kv_ref, whole, sems = refs
    copies = fetches(here_ref, (mine_ref, other_ref), whole, sems)
    stacked((kv0, kv1, kv2, kv3), kv_ref)
    width = q_ref.shape[1]
    visible = pk_ref[...] <= pq_ref[...]
    for i in range(width // HEAD):
        h = slice(i * HEAD, (i + 1) * HEAD)
        scores = masked_scores(q_ref[:, h], kv_ref[:, h], visible)
        most = jnp.max(scores, -1, keepdims=True)
        exponent = jnp.exp(scores - most)
        total = jnp.sum(exponent, -1, keepdims=True)
        probs = (exponent / total).astype(BF)
        values = kv_ref[:, width + i * HEAD : width + (i + 1) * HEAD]
        mixed_ref[:, h] = dot(probs, values).astype(BF)
        lse_ref[:, h] = jnp.broadcast_to(most + jnp.log(total), (q_ref.shape[0], HEAD))
    fetched(copies)
    store_parts(dot(mixed_ref[...], whole[...]), part_refs)


def attend_back_kernel(
    here_ref, b0, b1, b2, b3, q_ref, kv0, kv1, kv2, kv3, lse_ref, pq_ref, pk_ref, cos_ref, sin_ref,
    mine_ref, other_ref, b_ref, dq_ref, own_ref, send_ref, far_ref, kv_ref, whole, sems,
):
    copies = fetches(here_ref, (mine_ref, other_ref), whole, sems)
    stacked((b0, b1, b2, b3), b_ref)
    stacked((kv0, kv1, kv2, kv3), kv_ref)
    fetched(copies)
    tokens, width = q_ref.shape
    scale = 1.0 / math.sqrt(HEAD)
    visible = pk_ref[...] <= pq_ref[...]
    grad_mixed = dot_t(b_ref[...], whole[...]).astype(BF)
    for i in range(width // HEAD):
        h = slice(i * HEAD, (i + 1) * HEAD)
        vh = slice(width + i * HEAD, width + (i + 1) * HEAD)
        q, k, v, g = q_ref[:, h], kv_ref[:, h], kv_ref[:, vh], grad_mixed[:, h]
        probs = jnp.exp(masked_scores(q, k, visible) - lse_ref[:, i * HEAD : i * HEAD + 1])
        grad_probs = dot_t(g, v)
        weighted = jnp.sum(probs * grad_probs, -1, keepdims=True)
        grad_scores = (probs * (grad_probs - weighted)).astype(BF)
        dq = dot(grad_scores, k) * scale
        dq_ref[:, h] = (dq * cos_ref[...] - swap_halves(dq) * sin_ref[...]).astype(BF)
        for lanes, grad in (
            (h, t_dot(grad_scores, q) * scale),
            (vh, t_dot(probs.astype(BF), g)),
        ):
            own_ref[:, lanes] = grad[:tokens]
            send_ref[:tokens, lanes] = grad[tokens : 2 * tokens].astype(BF)
            far_ref[:, lanes] = grad[2 * tokens : 3 * tokens].astype(BF)
            send_ref[tokens:, lanes] = grad[3 * tokens :].astype(BF)


def project_back_kernel(here_ref, dq_ref, own_ref, near_ref, far_ref, cos_ref, sin_ref, *refs):
    *refs, grad_ref, p0, p1, p2, p3, whole, sems = refs
    part_refs = (p0, p1, p2, p3)
    copies = fetches(here_ref, refs, whole, sems)
    width = dq_ref.shape[1]
    grad_ref[:, :width] = dq_ref[...]
    for h in range(0, 2 * width, HEAD):
        lanes = slice(h, h + HEAD)
        near = near_ref[: dq_ref.shape[0], lanes]
        v = own_ref[:, lanes] + near.astype(F32) + far_ref[:, lanes].astype(F32)
        if h < width:
            v = v * cos_ref[...] - swap_halves(v) * sin_ref[...]
        grad_ref[:, width + h : width + h + HEAD] = v.astype(BF)
    fetched(copies)
    store_parts(dot_t(grad_ref[...], whole[...]), part_refs)


def feed_kernel(
    here_ref, n0, n1, n2, n3, mask_ref, mine_ref, other_ref, n_ref, act_ref, slope_ref, *refs
):
    *part_refs, whole, sems = refs
    units = act_ref.shape[1]
    pair = (mine_ref, other_ref)
    ups = fetches(here_ref, pair, whole, sems.at[pl.ds(0, 16)], slice(0, units))
    downs = fetches(here_ref, pair, whole, sems.at[pl.ds(16, 16)], slice(units, None))
    stacked((n0, n1, n2, n3), n_ref)
    fetched(ups)
    step = units // 4
    for at in range(0, units, step):
        lanes = slice(at, at + step)
        value, slope = gelu_parts(dot(n_ref[...], whole[:, lanes]))
        act_ref[:, lanes] = (value * mask_ref[:, lanes]).astype(BF)
        slope_ref[:, lanes] = slope * mask_ref[:, lanes]
    fetched(downs)
    store_parts(dot(act_ref[...], whole[:, units:]), part_refs)


def feed_back_kernel(
    here_ref, b0, b1, b2, b3, slope_ref, mine_ref, other_ref, b_ref, grad_ref, *refs
):
    *part_refs, whole, sems = refs
    units = grad_ref.shape[1]
    pair = (mine_ref, other_ref)
    downs = fetches(here_ref, pair, whole, sems.at[pl.ds(16, 16)], slice(units, None))
    ups = fetches(here_ref, pair, whole, sems.at[pl.ds(0, 16)], slice(0, units))
    stacked((b0, b1, b2, b3), b_ref)
    fetched(downs)
    grad_ref[...] = (dot_t(b_ref[...], whole[:, units:]) * slope_ref[...]).astype(BF)
    fetched(ups)
    store_parts(dot_t(grad_ref[...], whole[:, :units]), part_refs)


def feed_both_kernel(
    here_ref, n0, n1, n2, n3, mask_ref, b_ref, mine_ref, other_ref, n_ref, act_ref, grad_ref, *refs
):
    *part_refs, slope_ref, whole, sems = refs
    units = act_ref.shape[1]
    pair = (mine_ref, other_ref)
    ups = fetches(here_ref, pair, whole, sems.at[pl.ds(0, 16)], slice(0, units))
    downs = fetches(here_ref, pair, whole, sems.at[pl.ds(16, 16)], slice(units, None))
    stacked((n0, n1, n2, n3), n_ref)
    fetched(ups)
    step = units // 4
    for at in range(0, units, step):
        lanes = slice(at, at + step)
        value, slope = gelu_parts(dot(n_ref[...], whole[:, lanes]))
        act_ref[:, lanes] = (value * mask_ref[:, lanes]).astype(BF)
        slope_ref[:, lanes] = slope * mask_ref[:, lanes]
    fetched(downs)
    grad_ref[...] = (dot_t(b_ref[...], whole[:, units:]) * slope_ref[...]).astype(BF)
    store_parts(dot_t(grad_ref[...], whole[:, :units]), part_refs[4:])
    store_parts(dot(act_ref[...], whole[:, units:]), part_refs[:4])


def block_grads(refs):
    for i in range(len(refs) // 4):
        left, left_near, right, right_near = refs[4 * i : 4 * i + 4]
        total = t_dot(left[...], right[...]) + t_dot(left_near[...], right_near[...])
        yield i, total.reshape(4, total.shape[0] // 4, total.shape[1])


def weight_grad_kernel(here_ref, *refs):
    *refs, out_ref = refs
    done = 0
    for i, total in block_grads(refs[: len(refs) // 4 * 4]):
        rows = total.shape[1]
        out_ref[:, 0, done : done + rows] = total.astype(BF)
        done += rows
    for ref in refs[len(refs) // 4 * 4 :]:
        out_ref[:, 0, done:] = ref[:, 0]


def weight_grads(here, groups, below=()):
    tokens, features = groups[0][0].shape
    columns = groups[0][2].shape[1]
    rows = features // 16 * len(groups) + sum(a.shape[2] for a in below)
    args = [a for group in groups for a in group]
    by_xh = lambda n: pl.BlockSpec((4, 1, n, columns), lambda i, here: (0, i, 0, 0))
    left = pl.BlockSpec((tokens, features // 4), lambda i, here: (0, 2 * i + here[0]))
    right = pl.BlockSpec((tokens, columns), lambda i, here: (0, 0))
    return pl.pallas_call(
        weight_grad_kernel,
        grid_spec=pltpu.PrefetchScalarGridSpec(
            num_scalar_prefetch=1,
            grid=(2,),
            in_specs=[left, left, right, right] * len(groups) + [by_xh(a.shape[2]) for a in below],
            out_specs=by_xh(rows),
        ),
        out_shape=shape((4, 2, rows, columns), BF),
        compiler_params=pltpu.CompilerParams(vmem_limit_bytes=56 * 2**20),
        cost_estimate=LIGHT,
    )(here, *args, *below)


def near(array):
    return shifted(array, "core", 1)


def with_near(arrays):
    return [*arrays, *(near(a) for a in arrays)]


def layer_pairs(shard):
    sec = lax.axis_index("sec")
    places = [(sec, xh) for sec in (0, 1) for xh in (0, 1)]
    across = [(2 * s + x, 2 * (1 - s) + 1 - x) for s, x in places]
    own = jnp.stack([shard, shifted(shard, "xh", 1)])
    other = jnp.stack([shifted(shard, "sec", 1), lax.ppermute(shard, ("sec", "xh"), across)])
    return jnp.where(sec == 0, own, other), jnp.where(sec == 0, other, own)


def y_gathered(pair):
    return lax.all_gather(pair, "y", axis=0, tiled=False)


def scaled(v):
    return (v * norm_scale(v)).astype(BF)


def attention(x, normed, w_out, tables, hook):
    cos, sin, pos_here, pos_whole, unit_mask, here = tables
    x = x.astype(F32)
    w_in, normed = hook(0, normed)
    tokens, features = 4 * x.shape[0], x.shape[1]
    width = w_in[0].shape[-1] // 3
    normed, queries, kv = call(
        qkv_kernel,
        [shape((tokens, features), BF), shape((tokens, width), BF), shape((tokens, 2 * width), BF)],
        here, *normed, cos, sin, rows=features, blocks=w_in,
    )
    kv = hook(1, kv)
    kv = family(kv)
    kv = hook(2, kv)
    mixed, lse, *parts = call(
        attend_kernel,
        [shape((tokens, width), BF), shape((tokens, width), F32), *part_shapes(features)],
        here, queries, *kv, pos_here, pos_whole, rows=width, blocks=w_out(),
        scratch=[pltpu.VMEM((4 * tokens, 2 * width), BF)],
    )
    parts = hook(3, parts)
    received = hook(7, sent_home(parts))
    middle = x + summed(parts, received)
    return middle, (x, queries, kv, lse, middle), [(a, near(a)) for a in (normed, mixed)], w_in


def lefts_of(normed, activated):
    return [(a, near(a)) for a in (normed, activated)]


def feed_shapes(features, mask, *types):
    by_unit = [shape((256, mask.shape[1]), t) for t in types]
    return [shape((256, features), BF), *by_unit, *part_shapes(features)]


def arrived(middle, parts, received):
    return (middle + summed(parts, received)).astype(BF)


def norm_backward(v, q, straight):
    scale = norm_scale(v)
    n = v * scale
    return straight + scale * (q - n * jnp.mean(q * n, -1, keepdims=True))


def backward(grad_out, branch, kept, feed_back, lefts, weights, tables, hook, last):
    x, queries, kv, lse, middle = kept
    normed, mixed, normed_two, activated = lefts
    w_in, w_out = weights
    cos, sin, pos_here, pos_whole, unit_mask, here = tables
    tokens, width = queries.shape
    features = x.shape[1]
    grad_out = grad_out.astype(F32)
    grad_up, *parts = feed_back
    received = sent_home(parts)
    feed = weight_grads(
        here,
        [(*normed_two, grad_up, near(grad_up)), (*activated, branch, near(branch))],
    )
    received, feed = tied(received, feed)
    received = hook(1, received, feed)
    grad_middle = norm_backward(middle, summed(parts, received), grad_out)
    ring = gather_ring(grad_middle.astype(BF), "z")
    ring = hook(2, ring)
    branch, dq, own, send, far = call(
        attend_back_kernel,
        [
            shape((tokens, features), BF),
            shape((tokens, width), BF),
            shape((tokens, 2 * width), F32),
            shape((2 * tokens, 2 * width), BF),
            shape((tokens, 2 * width), BF),
        ],
        here, *ring, queries, *kv, lse, pos_here, pos_whole, cos, sin, rows=width, blocks=w_out,
        scratch=[pltpu.VMEM((4 * tokens, 2 * width), BF)],
    )
    dq, own, send, far = hook(6, (dq, own, send, far))
    branch_near = near(branch)
    send = near(send)
    far = (far.astype(F32) + send[tokens:].astype(F32)).astype(BF)
    far = shifted(far, "sec", 1)
    out = t_dot(jnp.concatenate(mixed, 0), jnp.concatenate([branch, branch_near], 0)).astype(BF)
    out = lax.dynamic_index_in_dim(out.reshape(2, 2, -1, features), here[0], 1, keepdims=False)
    out = out.reshape(2, 4, -1, features).transpose(1, 0, 2, 3)
    out = out.reshape(4, 2, -1, 3 * width)
    far, out = tied(far, out)
    far = hook(3, far)
    grad_projected, *parts = call(
        project_back_kernel,
        [shape((tokens, 3 * width), BF), *part_shapes(features)],
        here, dq, own, send, far, cos, sin, rows=features, blocks=w_in,
    )
    parts, grad_projected = hook(5, (parts, grad_projected))
    g_in = weight_grads(here, [(*normed, grad_projected, near(grad_projected))], [out])
    if last:
        hook(4, None, g_in)
        received = sent_home(parts)
    else:
        received, g_in = tied(sent_home(parts), g_in)
        received = hook(4, received, g_in)
    return norm_backward(x, summed(parts, received), grad_middle).astype(BF)


def home_route():
    return [
        ((dp * 4 + y) * 4 + z, (y * 4 + z) * 4 + dp)
        for dp in range(4)
        for y in range(4)
        for z in range(4)
    ]


def local(
    inputs,
    cotangent,
    positions,
    granularity,
    attention_gain,
    attention_in,
    attention_out,
    feed_gain,
    feed_up,
    feed_down,
):
    sec = lax.axis_index("sec")
    rows, width_in = attention_in.shape[1:]
    model = attention_out.shape[2]
    units = feed_up.shape[2]

    core = lax.axis_index("core")

    def layered(mine):
        other = shifted(mine, "sec", 1)
        return jnp.where(sec == 0, mine, other), jnp.where(sec == 0, other, mine)

    def with_gain(weight, gain):
        return (weight.astype(F32) * gain.astype(F32)[:, None]).astype(BF)

    w_in = with_gain(attention_in[0], attention_gain[0])
    w_up = with_gain(feed_up[0], feed_gain[0])
    w_in = w_in.reshape(rows, 3, 4, width_in // 12).transpose(2, 0, 1, 3)
    w_up = w_up.reshape(rows, 16, 4, units // 64).transpose(2, 0, 1, 3)
    both = [w_in.reshape(4, rows, width_in // 4), w_up.reshape(4, rows, units // 4)]
    both = lax.all_to_all(jnp.concatenate(both, 2), "z", 0, 0, tiled=True)
    outs = lax.ppermute(attention_out[0], ("xh", "core", "y", "z"), home_route())
    streams = jnp.stack([inputs, cotangent], 1)
    both, streams, positions, outs = tied(both.reshape(4 * rows, -1), streams, positions, outs)
    attn = jnp.concatenate([both[:, : width_in // 4], outs.reshape(-1, width_in // 4)], 0)
    attn_0, attn_1 = layer_pairs(attn)
    streams = brought(streams)
    feed = jnp.concatenate([both[:, width_in // 4 :], feed_down[0]], 1)
    attn_0, attn_1, (x_0, cotangent) = tied(attn_0, attn_1, streams)
    attn_0 = y_gathered(attn_0)
    feed_0, feed_1 = layer_pairs(feed)
    ring = gather_ring(jnp.stack([scaled(x_0.astype(F32)), cotangent]), "z")
    feed_0, feed_1, ring = tied(feed_0, feed_1, ring)
    normed_0, branch_1 = ([a[i] for a in ring] for i in (0, 1))
    branch_1 = jnp.concatenate(branch_1, 0)
    feed_0 = y_gathered(feed_0)

    def out_rows(attn):
        out = attn[:, :, 4 * rows :].reshape(4, 2, rows, model)
        return with_near([out.transpose(1, 0, 2, 3).reshape(2, 4 * rows, model)])

    y = lax.axis_index("y")
    seq = lambda a: lax.dynamic_index_in_dim(a, y, 0, keepdims=False)
    facts = jnp.concatenate([positions, jnp.broadcast_to(granularity[:, None], (2, 128))], 1)
    other = shifted(facts, "core", 1)
    facts = jnp.where(core == 0, jnp.concatenate([facts, other]), jnp.concatenate([other, facts]))
    facts = seq(facts)
    level = facts[-1]
    pos = rolled(facts[:-128].reshape(2, 2, 4, -1), "z", 2)
    pos = rolled(rolled(pos, "core", 1), "sec", 0).reshape(4, -1)
    here = jnp.stack([core, y, lax.axis_index("xh"), 0])
    half = HEAD // 2
    freqs = jnp.exp(-math.log(THETA) * jnp.arange(half, dtype=F32) / half)
    angles = pos[0].astype(F32)[:, None] * freqs
    cos, sin = jnp.cos(angles), jnp.sin(angles)
    unit_width = (units // 32) * lax.shift_left(1, level)
    tables = (
        jnp.concatenate([cos, cos], 1),
        jnp.concatenate([-sin, sin], 1),
        pos[0][:, None],
        pos.reshape(1, -1),
        (jnp.arange(units // 4) < unit_width).astype(F32)[None],
        here,
    )

    at = {"attn_0": attn_0, "attn_1": attn_1, "feed_0": feed_0, "feed": feed_1}

    def hold(chain, *names):
        values = [at[n] for n in names]
        chain, values = tied(chain, values)
        at.update(zip(names, values))
        return chain

    def forward_0(point, chain, *more):
        if point == 0:
            chain = hold(chain, "attn_0")
            return with_near([at["attn_0"]]), chain
        if point == 1:
            at["out_0"] = out_rows(at["attn_0"])
        if point == 2:
            chain = hold(chain, "attn_1", "feed", "out_0")
            at["attn_1"], at["feed"] = y_gathered(at["attn_1"]), y_gathered(at["feed"])
        if point == 7:
            chain = hold(chain, "feed_0")
            at["feed_0"] = with_near([at["feed_0"]])
        if point == 8:
            chain = hold(chain, "attn_1")
            at["in_1"] = with_near([at["attn_1"]])
        return chain

    def forward_1(point, chain, *more):
        if point == 0:
            chain = hold(chain, "in_1")
            return at["in_1"], chain
        if point == 1:
            at["out_1"] = out_rows(at["attn_1"])
        if point == 2:
            chain = hold(chain, "out_1")
        if point == 7:
            chain = hold(chain, "feed")
            at["feed"] = with_near([at["feed"]])
        return chain

    mask = tables[4]
    middle_0, kept_0, lefts_0, in_0 = attention(
        x_0, normed_0, lambda: at["out_0"], tables, forward_0
    )
    normed = forward_0(4, gather_ring(scaled(middle_0), "z"))
    feed_0 = at["feed_0"]
    normed, activated, slope_0, *parts = call(
        feed_kernel, feed_shapes(model, mask, BF, F32), here, *normed, mask, rows=model, blocks=feed_0
    )
    lefts_0 += lefts_of(normed, activated)
    hidden_0 = forward_0(8, arrived(middle_0, parts, sent_home(parts)))
    middle_1, kept_1, lefts_1, in_1 = attention(
        hidden_0, gather_ring(scaled(hidden_0.astype(F32)), "z"), lambda: at["out_1"], tables, forward_1
    )
    normed = forward_1(4, gather_ring(scaled(middle_1), "z"))
    normed, activated, grad_up, *parts = call(
        feed_both_kernel,
        feed_shapes(model, mask, BF, BF) + part_shapes(model),
        here, *normed, mask, branch_1, rows=model, blocks=at["feed"],
        scratch=[pltpu.VMEM((256, mask.shape[1]), F32)],
    )
    lefts_1 += lefts_of(normed, activated)
    parts_1, feed_back_1 = parts[:4], [grad_up, *parts[4:]]
    out_0, out_1 = at["out_0"], at["out_1"]

    def y_sum(grads):
        flat = grads.reshape(-1, grads.shape[-1])
        flat = lax.psum_scatter(flat, "y", scatter_dimension=0, tiled=True)
        return flat.reshape(grads.shape[1:])

    def x_terms(blocks):
        xh = here[2]
        pick = lambda l, x: lax.dynamic_index_in_dim(
            lax.dynamic_index_in_dim(blocks, l, 0, keepdims=False), x, 0, keepdims=False
        )
        places = [(a, x) for a in (0, 1) for x in (0, 1)]
        across = [(2 * a + x, 2 * (1 - a) + 1 - x) for a, x in places]
        return [
            pick(sec, xh),
            shifted(pick(sec, 1 - xh), "xh", 1),
            shifted(pick(1 - sec, xh), "sec", 1),
            lax.ppermute(pick(1 - sec, 1 - xh), ("sec", "xh"), across),
        ]

    def terms(blocks):
        return sum(a.astype(F32) for a in blocks)

    at["parts"] = parts_1

    def backward_1(point, chain, *grads):
        if point == 1:
            at["feed1"] = y_sum(grads[0])
        if point == 2:
            chain = hold(chain, "parts")
            at["received"] = sent_home(at["parts"])
        if point == 3:
            chain = hold(chain, "received")
        if point == 4:
            chain = hold(chain, "feed1")
            at["in1"] = y_sum(grads[0])
        return chain

    def backward_0(point, chain, *grads):
        if point == 1:
            chain = hold(chain, "in1")
            at["feed0"] = y_sum(grads[0])
        if point == 5:
            chain = hold(chain, "feed0")
            feeds = jnp.stack([at["feed0"], at["feed1"]])
            at["up"] = x_terms(feeds[:, :, : 4 * rows])
            at["up"][1], down = tied(at["up"][1], feeds[:, :, 4 * rows :])
            at["down"] = x_terms(down)
        if point == 4:
            g_in, at["to_1"] = tied(grads[0], at["to_1"])
            at["in0"] = y_sum(g_in)
        return chain

    grad_1 = backward(
        cotangent, branch_1, kept_1, feed_back_1, lefts_1, (in_1, out_1), tables, backward_1, False
    )
    hidden_1 = arrived(middle_1, at["parts"], at["received"])
    at["to_1"] = jnp.stack([hidden_1, grad_1])
    branch_0, *feed_back_0 = call(
        feed_back_kernel,
        feed_shapes(model, mask, BF),
        here, *gather_ring(grad_1, "z"), slope_0, rows=model, blocks=feed_0,
    )
    grad_0 = backward(
        grad_1, branch_0, kept_0, feed_back_0, lefts_0, (in_0, out_0), tables, backward_0, True
    )
    def columns_home(block):
        z = lax.axis_index("z")
        pick = lambda k: lax.dynamic_index_in_dim(block, lax.rem(z + k, 4), 0, keepdims=False)
        got = [pick(0)] + [shifted(pick(k), "z", k) for k in (1, 2, 3)]
        return rolled(jnp.stack(got), "z", 0)

    g_up = columns_home(terms(at["up"]).astype(BF).reshape(4, rows, -1))
    g_in, g_out = (
        jnp.stack([at[n][:, rows_of] for n in ("in0", "in1")])
        for rows_of in (slice(0, 4 * rows), slice(4 * rows, None))
    )
    g_in = lax.all_to_all(g_in.reshape(16, rows, -1), ("sec", "xh", "z"), 0, 0, tiled=True)
    g_out = terms(x_terms(g_out.reshape(2, 2, rows, model)))
    g_in, grad_0, g_up, at["down"] = tied(g_in, grad_0, g_up, at["down"])
    g_up, g_down = g_up.astype(F32), terms(at["down"])
    g_in = jnp.sum(g_in.reshape(4, 4, rows, -1).astype(F32), 0)
    to_0 = returned(jnp.stack([hidden_0, grad_0]), 0)
    to_1 = returned(at["to_1"], 1)
    hidden, input_grads = (jnp.where(sec == 0, a, b)[None] for a, b in zip(to_0, to_1))
    g_in = g_in.reshape(4, rows, 3, width_in // 12).transpose(1, 2, 0, 3).reshape(rows, width_in)
    g_up = g_up.reshape(4, rows, 16, units // 64).transpose(1, 2, 0, 3).reshape(rows, units)
    back = [(b, a) for a, b in home_route()]
    g_out = lax.ppermute(g_out.astype(BF), ("xh", "core", "y", "z"), back).astype(F32)


    def home(grad, weight, gain):
        return grad * gain.astype(F32)[:, None], jnp.sum(grad * weight.astype(F32), 1)

    g_in, g_gain = home(g_in, attention_in[0], attention_gain[0])
    g_up, g_gain_two = home(g_up, feed_up[0], feed_gain[0])
    return (
        hidden,
        input_grads,
        g_gain[None],
        g_in[None],
        g_out[None],
        g_gain_two[None],
        g_up[None],
        g_down[None],
    )


def solution(mesh):
    fine = Mesh(mesh.devices.reshape(2, 2, 2, 4, 4), EVERY)
    dp, ctx = ("xh", "core"), ("y", "z")
    ranks = dp + ctx
    in_specs = (
        P(dp, ctx, None),
        P(dp, ctx, None),
        P(dp, None),
        P(dp),
        P("sec", ranks),
        P("sec", ranks, None),
        P("sec", ranks, None),
        P("sec", ranks),
        P("sec", ranks, None),
        P("sec", ranks, None),
    )
    out_specs = (
        P("sec", dp, ctx, None),
        P("sec", dp, ctx, None),
        P("sec", ranks),
        P("sec", ranks, None),
        P("sec", ranks, None),
        P("sec", ranks),
        P("sec", ranks, None),
        P("sec", ranks, None),
    )
    return jax.shard_map(local, mesh=fine, in_specs=in_specs, out_specs=out_specs, check_vma=False)
```
